32 devices in a mesh: groups: 2 (over x), ctx: 16 (over z, y, core).
Axes of the slice: x: 2, y: 2, z: 4, core: 2. Of those that a mesh axis runs over, the one named last changes fastest.
Arguments:
- hidden: bfloat16 [256, 8192], P('groups', 'ctx'), parts along dimension 0, may hold values from -6 to 6
- attn_gain: bfloat16 [8192], P('ctx'), may hold values from 0.25 to 1.75
- q_weight: bfloat16 [8192, 8192], P(None, 'ctx'), may hold values from -0.0625 to 0.0625
- q_gain: bfloat16 [128], replicated, may hold values from 0.25 to 1.75
- key_cache: bfloat16 [49152, 1024], P(('groups', 'ctx')), parts along dimension 0, may hold values from -64 to 64
- value_cache: bfloat16 [49152, 1024], P(('groups', 'ctx')), parts along dimension 0, may hold values from -6 to 6
- block_limit: int32 [256], P('groups'), parts along dimension 0, may hold values from 0 to 191, as said below
- out_weight: bfloat16 [8192, 8192], P('ctx'), may hold values from -0.09375 to 0.09375
- next_gain: bfloat16 [8192], P('ctx'), may hold values from 0.25 to 1.75
- next_weight: bfloat16 [8192, 8192], P(None, 'ctx'), may hold values from -0.0625 to 0.0625
Outputs:
- new_hidden: bfloat16 [256, 8192], P('groups', 'ctx'), parts along dimension 0
- next_queries: bfloat16 [256, 8192], P('groups', 'ctx'), parts along dimension 0
The draws below stay inside these ranges and needn't reach their ends.
There are 2 independent parts, one for each index of `groups`. The reference program is written for one: setup_inputs(seed, part) draws one part's arguments, and reference() takes and returns one part's arrays. A program takes and returns all parts, laid end to end along the dimension named above; an argument that names none is the same for every part. Nothing has to cross between parts.
Inputs may be any that keep to these rules, and one draw needn't show every extreme that they name: Text token i may attend the visual blocks 0 to block_limit[i], each of 128 visual tokens; some token reaches the last block and some only the first.
All inputs are finite; a program needn't handle non-finite values.
Results may differ from the reference program's by a relative error of at most 0.015.
Values may be sent and summed in bfloat16 or wider, within the bound.
No kernel may reach another device: no remote copies, remote signals or barrier semaphores. Data moves between devices by JAX's collectives and lax.ppermute only.
A program may use at most 64 MiB of HBM per device.

```python
import jax
import jax.numpy as jnp
from jax import lax

D = 8192
HEADS = 64
KV_HEADS = 8
HEAD_DIM = 128
QUERIES = 128
BLK = 128
V_TOTAL = 24576
BLOCKS = 192


def draw_key_cache(key, part):
    first_key = jax.random.fold_in(jax.random.fold_in(key, 11), 0)
    shape = (V_TOTAL, KV_HEADS * HEAD_DIM)
    base = 3.0 * jax.random.truncated_normal(first_key, -6.0, 6.0, shape, jnp.float32)
    return base.astype(jnp.bfloat16)


def draw_block_limit(key, part):
    first_key, second_key, third_key = jax.random.split(jax.random.fold_in(key, 23), 3)
    limits = jax.random.randint(first_key, (QUERIES,), 0, BLOCKS)
    highest = jax.random.randint(second_key, (), 0, QUERIES)
    lowest = (highest + 1 + jax.random.randint(third_key, (), 0, QUERIES - 1)) % QUERIES
    limits = limits.at[highest].set(BLOCKS - 1).at[lowest].set(0)
    return limits.astype(jnp.int32)


def spiked(array, rng, source, target, shards_of, factor):
    def block_of(axis_at):
        return (jnp.arange(array.shape[axis_at]) // (array.shape[axis_at] // shards_of)).reshape((-1,) + (1,) * (array.ndim - 1 - axis_at))

    one_side = jax.random.permutation(rng, shards_of)[block_of(target)]
    far = (block_of(target) + shards_of // 2) % shards_of
    return jnp.where((block_of(source) == one_side) | (block_of(source) == far), factor * array, array)


def levels(key, extent, shards, low, top_value):
    loudness = 1.0
    for dim, blocks in shards:
        steps = jax.random.uniform(jax.random.fold_in(jax.random.fold_in(key, 6), dim), (blocks,), jnp.float32, low / len(shards), top_value / len(shards))
        loudness = loudness * jnp.repeat(jnp.exp(steps), extent[dim] // blocks).reshape((-1,) + (1,) * (len(extent) - 1 - dim))
    return loudness


def noise(stream_key, dims, scale, most, cuts=(), kind=jnp.bfloat16):
    values = jax.random.normal(stream_key, dims, jnp.float32) * scale
    if len(cuts) > 0:
        values = levels(stream_key, dims, cuts, -0.22, 0.18) * values
    return jnp.clip(values, min=-most, max=most).astype(kind)


def gaussian_with(key, extent, width, bound, pieces, heavy, held_as=jnp.bfloat16):
    entries = width * jax.random.normal(key, extent, jnp.float32)
    if pieces:
        entries = entries * levels(key, extent, pieces, -0.22, 0.18)
    return jnp.clip(spiked(entries, jax.random.fold_in(key, 3), *heavy), -bound, bound).astype(held_as)


def setup_inputs(seed: int = 0, part: int = 0) -> dict:
    seeds = jax.random.split(jax.random.key(seed), 11)
    part_splits = jax.random.split(jax.random.fold_in(seeds[10], part), 11)
    hidden = noise(part_splits[0], (QUERIES, D), 1.0, 6.0, ((1, 16),))
    attn_gain = jnp.clip(1.0 + 0.15 * jax.random.normal(seeds[1], (D,), jnp.float32), 0.25, 1.75).astype(jnp.bfloat16)
    q_weight = noise(seeds[2], (D, HEADS * HEAD_DIM), D ** -0.5, 0.0625, ((1, 16),))
    q_gain = jnp.clip(1.0 + 0.15 * jax.random.normal(seeds[3], (HEAD_DIM,), jnp.float32), 0.25, 1.75).astype(jnp.bfloat16)
    key_cache = draw_key_cache(jax.random.fold_in(jax.random.fold_in(seeds[10], part), 71), part)
    value_cache = noise(part_splits[5], (V_TOTAL, KV_HEADS * HEAD_DIM), 1.0, 6.0, ((0, 16),))
    block_limit = draw_block_limit(jax.random.fold_in(jax.random.fold_in(seeds[10], part), 71), part)
    out_weight = gaussian_with(seeds[7], (HEADS * HEAD_DIM, D), (HEADS * HEAD_DIM) ** -0.5, 0.09375, ((0, 16),), (0, 1, 16, 2.0))
    next_gain = jnp.clip(1.0 + 0.15 * jax.random.normal(seeds[8], (D,), jnp.float32), 0.25, 1.75).astype(jnp.bfloat16)
    next_weight = noise(seeds[9], (D, HEADS * HEAD_DIM), D ** -0.5, 0.0625, ((1, 16),))
    return {"hidden": hidden, "attn_gain": attn_gain, "q_weight": q_weight, "q_gain": q_gain, "key_cache": key_cache, "value_cache": value_cache, "block_limit": block_limit, "out_weight": out_weight, "next_gain": next_gain, "next_weight": next_weight}


def rms_rows(rows_in, gain):
    values = rows_in.astype(jnp.float32)
    square_mean = lax.optimization_barrier(jnp.mean(values * values, axis=-1, keepdims=True))
    return (values * lax.rsqrt(square_mean + 1e-05) * gain.astype(jnp.float32)).astype(jnp.bfloat16)

def reference(hidden, attn_gain, q_weight, q_gain, key_cache, value_cache, block_limit, out_weight, next_gain, next_weight):
    normed = rms_rows(hidden, attn_gain)
    query = jnp.dot(normed, q_weight, preferred_element_type=jnp.float32)
    query = query.reshape(QUERIES, HEADS, HEAD_DIM)
    head_mean = lax.optimization_barrier(jnp.mean(query * query, axis=-1, keepdims=True))
    query_normed = (query * lax.rsqrt(head_mean + 1e-05) * q_gain.astype(jnp.float32)).astype(jnp.bfloat16)
    positions = jnp.arange(V_TOTAL, dtype=jnp.int32) // BLK
    allowed = positions[None, :] <= block_limit[:, None]
    scale = HEAD_DIM ** (-0.5)
    per_group = HEADS // KV_HEADS

    def one_head(head):
        group = (head // per_group).astype(jnp.int32)
        keys = lax.dynamic_slice_in_dim(key_cache, group * HEAD_DIM, HEAD_DIM, 1)
        values = lax.dynamic_slice_in_dim(value_cache, group * HEAD_DIM, HEAD_DIM, 1)
        single = lax.dynamic_index_in_dim(query_normed, head, 1, keepdims=False)
        scores = jnp.dot(single, keys.T, preferred_element_type=jnp.float32) * scale
        scores = jnp.where(allowed, scores, -jnp.inf)
        top = lax.optimization_barrier(jnp.max(scores, axis=-1, keepdims=True))
        expo = jnp.exp(scores - top)
        denominator = lax.optimization_barrier(jnp.sum(expo, axis=-1, keepdims=True))
        summed = jnp.dot(expo.astype(jnp.bfloat16), values, preferred_element_type=jnp.float32)
        return (summed / denominator).astype(jnp.bfloat16)
    attended = lax.map(one_head, jnp.arange(HEADS, dtype=jnp.int32))
    attended = jnp.transpose(attended, (1, 0, 2)).reshape(QUERIES, HEADS * HEAD_DIM)
    mixed = jnp.dot(attended, out_weight, preferred_element_type=jnp.float32)
    new_hidden = (hidden.astype(jnp.float32) + mixed).astype(jnp.bfloat16)
    renormed = rms_rows(new_hidden, next_gain)
    next_queries = jnp.dot(renormed, next_weight, preferred_element_type=jnp.float32).astype(jnp.bfloat16)
    return (new_hidden, next_queries)
```

```python
import functools
import math

import jax
import jax.numpy as jnp
from jax import lax
from jax.experimental import pallas as pl
from jax.experimental.pallas import tpu as pltpu
from jax.sharding import PartitionSpec as P

BLK = 128
EPSILON = 1e-05
MASKED = -1e30
LANES = 128
TILE = 16
BF16 = jnp.bfloat16
F32 = jnp.float32
VMEM = pl.BlockSpec(memory_space=pltpu.VMEM)
ANYWHERE = pl.BlockSpec(memory_space=pl.ANY)
SCALARS = pl.BlockSpec(memory_space=pltpu.SMEM)


class Ring:
    def __init__(self, devices, columns):
        self.chips = devices // 2
        if columns == 2 and self.chips % 2 == 0:
            self.order = list(range(0, self.chips, 2)) + list(range(1, self.chips, 2))[::-1]
        else:
            self.order = list(range(self.chips))
        self.snake = columns == 2 and self.chips % 2 == 0
        self.device = lax.axis_index("ctx")
        self.core = self.device % 2
        self.chip = self.device // 2
        if self.snake:
            self.place = jnp.where(
                self.chip % 2 == 0, self.chip // 2, self.chips - 1 - self.chip // 2
            )
        else:
            self.place = self.chip
        self.sign = 1 - 2 * self.core

    def owner(self, rounds):
        place = (self.place - self.sign * rounds + self.chips) % self.chips
        if not self.snake:
            return place
        half = self.chips // 2
        return jnp.where(place < half, 2 * place, 2 * (self.chips - 1 - place) + 1)

    def send(self, block, step):
        route = []
        for place in range(self.chips):
            for core in (0, 1):
                to = self.order[(place + (step if core == 0 else -step)) % self.chips]
                route.append((self.order[place] * 2 + core, to * 2 + core))
        return lax.ppermute(block, "ctx", sorted(route))

    def swap(self, block):
        return lax.ppermute(block, "ctx", [(i, i ^ 1) for i in range(2 * self.chips)])

    def in_order(self, own, other, axis):
        first = jnp.where(self.core == 0, own, other)
        second = jnp.where(self.core == 0, other, own)
        return jnp.concatenate([first, second], axis=axis)


def stat_rows(rows):
    return -(-3 * (rows // LANES) // TILE) * TILE


def diagonal():
    shape = (LANES, LANES)
    return lax.broadcasted_iota(jnp.int32, shape, 0) == lax.broadcasted_iota(jnp.int32, shape, 1)


def pack_stats(stats):
    high = [x.astype(BF16).astype(F32) for x in stats]
    rest = [x - h for x, h in zip(stats, high)]
    middle = [x.astype(BF16).astype(F32) for x in rest]
    low = [x - h for x, h in zip(rest, middle)]
    parts = high + middle + low
    parts += [jnp.zeros_like(stats[0])] * (-len(parts) % TILE)
    return jnp.concatenate(parts, axis=0).astype(BF16)


def unpack_stats(packed, blocks):
    packed = packed.astype(F32)
    return packed[:blocks] + packed[blocks : 2 * blocks] + packed[2 * blocks : 3 * blocks]


def attend_kernel(chunk, group, q, bias, k0, k1, v0, v1, out, kbuf, vbuf, sems):
    tokens = k0.shape[0]
    rows = q.shape[0]
    columns = pl.ds(pl.multiple_of(group[0] * LANES, LANES), LANES)
    copies = []
    for i, (source, buffer) in enumerate(((k0, kbuf), (k1, kbuf), (v0, vbuf), (v1, vbuf))):
        copy = pltpu.make_async_copy(
            source.at[:, columns],
            buffer.at[pl.ds((i % 2) * tokens, tokens), pl.ds(0, LANES)],
            sems.at[i],
        )
        copy.start()
        copies.append(copy)
    shape = (2 * tokens, LANES)
    block = lax.broadcasted_iota(jnp.int32, shape, 0) // BLK
    lane = lax.broadcasted_iota(jnp.int32, shape, 1)
    kbuf[:, LANES:] = (block == lane).astype(F32).astype(BF16)
    vbuf[:, LANES:] = jnp.ones(shape, BF16)
    for copy in copies:
        copy.wait()
    diag = diagonal()
    biases = jnp.concatenate([bias[...]] * (chunk // bias.shape[0]), axis=0)
    stats = []
    for start in range(0, rows, chunk):
        query = jnp.concatenate([q[pl.ds(start, chunk), :], biases], axis=1)
        scores = lax.dot_general(
            query, kbuf[...], (((1,), (1,)), ((), ())), preferred_element_type=F32
        )
        peak = jnp.max(scores, axis=1, keepdims=True)
        weights = jnp.exp2(scores - peak).astype(BF16)
        sums = jnp.dot(weights, vbuf[...], preferred_element_type=F32)
        total = sums[:, LANES:]
        out[pl.ds(start, chunk), :] = (sums[:, :LANES] / total).astype(BF16)
        level = peak + jnp.log2(total)
        for b in range(chunk // LANES):
            part = level[b * LANES : (b + 1) * LANES]
            stats.append(jnp.sum(jnp.where(diag, part, 0.0), axis=0, keepdims=True))
    out[pl.ds(rows, stat_rows(rows)), :] = pack_stats(stats)


def attend(group, q, bias, cache):
    rows, width = q.shape
    tokens = cache[0].shape[0]
    chunk = math.gcd(rows, 256)
    return pl.pallas_call(
        functools.partial(attend_kernel, chunk),
        out_shape=jax.ShapeDtypeStruct((rows + stat_rows(rows), width), BF16),
        in_specs=[SCALARS, VMEM, VMEM] + [ANYWHERE] * 4,
        out_specs=VMEM,
        scratch_shapes=[
            pltpu.VMEM((2 * tokens, 2 * LANES), BF16),
            pltpu.VMEM((2 * tokens, 2 * LANES), BF16),
            pltpu.SemaphoreType.DMA((4,)),
        ],
        compiler_params=pltpu.CompilerParams(vmem_limit_bytes=40 * 1024 * 1024),
        cost_estimate=pl.CostEstimate(
            flops=16 * rows * tokens * width,
            bytes_accessed=8 * tokens * width,
            transcendentals=2 * rows * tokens,
        ),
        name="attend",
    )(group, q, bias, *cache)


def merged(diag, one, one_stat, two, two_stat):
    peak = jnp.maximum(one_stat, two_stat)
    one_part, two_part = jnp.exp2(one_stat - peak), jnp.exp2(two_stat - peak)
    total = one_part + two_part
    share = jnp.sum(jnp.where(diag, one_part / total, 0.0), axis=1, keepdims=True)
    one, two = one.astype(F32), two.astype(F32)
    return two + share * (one - two), peak + jnp.log2(total)


def merge_kernel(one, two, out):
    rows = out.shape[0] * LANES // (LANES + 3)
    rows -= rows % LANES
    while rows + stat_rows(rows) > out.shape[0]:
        rows -= LANES
    blocks = rows // LANES
    one_rows = rows
    while one_rows + stat_rows(one_rows) > one.shape[0]:
        one_rows -= LANES
    one_blocks = one_rows // LANES
    diag = diagonal()
    one_stats = unpack_stats(one[pl.ds(one_rows, stat_rows(one_rows)), :], one_blocks)
    two_stats = unpack_stats(two[pl.ds(rows, stat_rows(rows)), :], blocks)
    stats = []
    for b in range(blocks):
        here = pl.ds(b * LANES, LANES)
        if b < one_blocks:
            value, stat = merged(
                diag, one[here, :], one_stats[b : b + 1], two[here, :], two_stats[b : b + 1]
            )
            out[here, :] = value.astype(BF16)
        else:
            out[here, :] = two[here, :]
            stat = two_stats[b : b + 1]
        stats.append(stat)
    out[pl.ds(rows, stat_rows(rows)), :] = pack_stats(stats)


def merge(one, two):
    return pl.pallas_call(
        merge_kernel,
        out_shape=jax.ShapeDtypeStruct(two.shape, BF16),
        in_specs=[VMEM, VMEM],
        out_specs=VMEM,
        cost_estimate=pl.CostEstimate(
            flops=8 * two.size, bytes_accessed=6 * two.size, transcendentals=0
        ),
        name="merge",
    )(one, two)


def finish_kernel(queries, mine, other, out):
    width = mine.shape[1]
    rows = out.shape[0] * out.shape[1] // width
    blocks = rows // LANES
    diag = diagonal()
    mine_stats = unpack_stats(mine[pl.ds(rows, stat_rows(rows)), :], blocks)
    other_stats = unpack_stats(other[pl.ds(rows, stat_rows(rows)), :], blocks)
    for b in range(blocks):
        far = (b + blocks // 2) % blocks
        value, _ = merged(
            diag,
            mine[pl.ds(b * LANES, LANES), :],
            mine_stats[b : b + 1],
            other[pl.ds(far * LANES, LANES), :],
            other_stats[far : far + 1],
        )
        for part in range(LANES // queries):
            head = (b * LANES) // queries + part
            out[:, pl.ds(head * width, width)] = value[
                part * queries : (part + 1) * queries
            ].astype(BF16)


def finish(queries, mine, other, heads):
    width = mine.shape[1]
    return pl.pallas_call(
        functools.partial(finish_kernel, queries),
        out_shape=jax.ShapeDtypeStruct((queries, heads * width), BF16),
        in_specs=[VMEM, VMEM],
        out_specs=VMEM,
        cost_estimate=pl.CostEstimate(
            flops=8 * mine.size, bytes_accessed=6 * mine.size, transcendentals=0
        ),
        name="finish",
    )(mine, other)


def gather_project(ring, block, gain_of, weight):
    width = block.shape[1]
    rows = block.shape[0]

    def add(sums, squares, part, start, gains):
        values = part.astype(F32)
        scaled = (values * gains.astype(F32)).astype(BF16)
        piece = lax.dynamic_slice_in_dim(weight, start, part.shape[1], 0)
        return (
            sums + jnp.dot(scaled, piece, preferred_element_type=F32),
            squares + jnp.sum(values * values, axis=1, keepdims=True),
        )

    sums = jnp.zeros((rows, weight.shape[1]), F32)
    squares = jnp.zeros((rows, 1), F32)
    sums, squares = add(sums, squares, block, ring.owner(0) * width, gain_of(0, None, block))
    rounds = ring.chips // 2
    travelling = block
    for step in range(1, rounds + 1):
        last = step == rounds
        if last:
            half = width // 2
            travelling = lax.dynamic_slice_in_dim(travelling, ring.core * half, half, 1)
        travelling = ring.send(travelling, 1)
        opposite = ring.swap(travelling)
        if last:
            base = ring.owner(rounds) * width
            near, far = ring.core * half, (1 - ring.core) * half
            sums, squares = add(sums, squares, travelling, base + near, gain_of(step, near, travelling))
            sums, squares = add(sums, squares, opposite, base + far, gain_of(step, far, opposite))
        else:
            sums, squares = add(
                sums, squares, travelling, ring.owner(step) * width, gain_of(step, None, travelling)
            )
            sums, squares = add(
                sums, squares, opposite, ring.owner(-step) * width, gain_of(-step, None, opposite)
            )
    factor = lax.rsqrt(squares / weight.shape[0] + EPSILON)
    return sums * factor


def layer(ring, hidden, gains, weights, q_gain, bias, cache):
    attn_gain, next_gain = gains
    q_weight, out_weight, other_weight, next_weight = weights
    queries, here = hidden.shape
    head_dim = q_gain.shape[0]
    heads_here = q_weight.shape[1] // head_dim
    chip_heads = 2 * heads_here
    kv_heads = cache[0].shape[1] // head_dim
    group_size = heads_here * 2 * ring.chips // kv_heads
    rounds = ring.chips // 2

    def gain_of(gain):
        def get(step, offset, part):
            owner = ring.owner(step)
            start = owner * 2 * here + (0 if offset is None else offset)
            return lax.dynamic_slice_in_dim(gain, start, part.shape[1], 0)[None, :]

        return get

    block = ring.in_order(hidden, ring.swap(hidden), 1)
    query = gather_project(ring, block, gain_of(attn_gain), q_weight)
    shaped = query.reshape(queries, heads_here, head_dim)
    mean = jnp.mean(shaped * shaped, axis=-1, keepdims=True)
    scale = head_dim**-0.5 * math.log2(math.e)
    normed = (
        shaped * lax.rsqrt(mean + EPSILON) * (q_gain.astype(F32) * scale)
    ).astype(BF16)
    own_heads = normed.transpose(1, 0, 2).reshape(heads_here * queries, head_dim)
    travelling = jnp.concatenate([own_heads, ring.swap(own_heads)], axis=0)

    def partial(step, rows):
        group = (ring.owner(step) * chip_heads // group_size).astype(jnp.int32)
        return attend(group[None], rows, bias, cache)

    partials = [partial(0, own_heads)]
    for step in range(1, rounds + 1):
        if step == rounds:
            travelling = travelling[: heads_here * queries]
        travelling = ring.send(travelling, 1)
        partials.append(partial(step, travelling))
    running = partials[rounds]
    for step in range(rounds - 1, 0, -1):
        running = merge(ring.send(running, -1), partials[step])
    running = ring.send(running, -1)
    running = merge(partials[0], running)
    attended = finish(queries, running, ring.swap(running), chip_heads)
    own, other = jnp.split(attended, 2, axis=1)

    def mix(rows, weight, start, size):
        piece = lax.dynamic_slice_in_dim(weight, start, size, 1)
        return jnp.dot(rows, piece, preferred_element_type=F32)

    def mixed(step):
        start, size = ring.owner(step) * 2 * here, 2 * here
        if step == rounds:
            start, size = start + ring.core * here, here
        return mix(own, out_weight, start, size) + mix(other, other_weight, start, size)

    running = mixed(rounds)
    for step in range(rounds - 1, -1, -1):
        got = ring.send(running.astype(BF16), -1).astype(F32)
        if step == rounds - 1:
            zero = jnp.zeros_like(got)
            got = ring.in_order(got, zero, 1)
        if step:
            running = got + mixed(step)
        else:
            running = got + mix(own, out_weight, ring.owner(0) * 2 * here, 2 * here)
    running = running.astype(BF16)
    total = running.astype(F32) + ring.swap(running).astype(F32)
    new_block = (block.astype(F32) + total).astype(BF16)
    new_hidden = lax.dynamic_slice_in_dim(new_block, ring.core * here, here, 1)
    following = gather_project(ring, new_block, gain_of(next_gain), next_weight)
    return new_hidden, following.astype(BF16)


def gather_small(ring, block):
    blocks = {}
    whole = jnp.zeros((block.shape[0], ring.chips * block.shape[1]), block.dtype)
    rounds = ring.chips // 2
    travelling = block
    whole = lax.dynamic_update_slice_in_dim(whole, block, ring.owner(0) * block.shape[1], 1)
    for step in range(1, rounds + 1):
        travelling = ring.send(travelling, 1)
        opposite = ring.swap(travelling)
        for at, part in ((step, travelling), (-step, opposite)):
            whole = lax.dynamic_update_slice_in_dim(whole, part, ring.owner(at) * block.shape[1], 1)
    return whole


def on_device(
    streams,
    columns,
    hidden,
    attn_gain,
    q_weight,
    q_gain,
    key_cache,
    value_cache,
    block_limit,
    out_weight,
    next_gain,
    next_weight,
):
    ring = Ring(lax.axis_size("ctx"), columns)
    queries = hidden.shape[0]
    small = jnp.stack([attn_gain, next_gain])
    small = ring.in_order(small, ring.swap(small), 1)
    gains = gather_small(ring, small)
    tokens = key_cache.shape[0]
    cache = (key_cache, ring.swap(key_cache), value_cache, ring.swap(value_cache))
    other_weight = ring.swap(out_weight)
    lanes = jnp.arange(LANES, dtype=jnp.int32)
    own_blocks = tokens // BLK
    block = jnp.where(
        lanes < own_blocks,
        ring.device * own_blocks + lanes,
        (ring.device + ring.sign) * own_blocks + lanes - own_blocks,
    )
    bias = jnp.where(block[None, :] <= block_limit[:, None], 0.0, MASKED).astype(BF16)
    weights = (q_weight, out_weight, other_weight, next_weight)
    size = queries // streams
    outs = [
        layer(
            ring,
            hidden[i * size : (i + 1) * size],
            (gains[0], gains[1]),
            weights,
            q_gain,
            bias[i * size : (i + 1) * size],
            cache,
        )
        for i in range(streams)
    ]
    return tuple(jnp.concatenate(parts, axis=0) for parts in zip(*outs))


def solution(mesh):
    in_specs = (
        P("groups", "ctx"),
        P("ctx"),
        P(None, "ctx"),
        P(),
        P(("groups", "ctx"), None),
        P(("groups", "ctx"), None),
        P("groups"),
        P("ctx", None),
        P("ctx"),
        P(None, "ctx"),
    )
    out_specs = (P("groups", "ctx"), P("groups", "ctx"))
    columns = 2 if mesh.shape["groups"] == 2 else 1
    return jax.shard_map(
        functools.partial(on_device, 1, columns),
        mesh=mesh,
        in_specs=in_specs,
        out_specs=out_specs,
        check_vma=False,
    )
```

```python
import functools
import math

import jax
import jax.numpy as jnp
from jax import lax
from jax.experimental import pallas as pl
from jax.experimental.pallas import tpu as pltpu
from jax.sharding import PartitionSpec as P

BLK = 128
EPSILON = 1e-05
MASKED = -1e30
LANES = 128
TILE = 16
BF16 = jnp.bfloat16
F32 = jnp.float32
VMEM = pl.BlockSpec(memory_space=pltpu.VMEM)
ANYWHERE = pl.BlockSpec(memory_space=pl.ANY)
SCALARS = pl.BlockSpec(memory_space=pltpu.SMEM)


FREE = pl.CostEstimate(flops=0, bytes_accessed=0, transcendentals=0)


class Ring:
    def __init__(self, devices, columns):
        self.chips = devices // 2
        self.rounds = self.chips // 2
        self.snake = columns == 2 and self.chips % 2 == 0
        if self.snake:
            self.order = list(range(0, self.chips, 2)) + list(range(1, self.chips, 2))[::-1]
        else:
            self.order = list(range(self.chips))

    def locate(self, key_share):
        device = lax.axis_index("ctx")
        core, chip = device % 2, device // 2
        half = self.chips // 2
        if self.snake:
            place = jnp.where(chip % 2 == 0, chip // 2, self.chips - 1 - chip // 2)
        else:
            place = chip
        names, values = ["self", "pair"], [device, device + 1 - 2 * core]
        for step in range(-self.rounds, self.rounds + 1):
            owner = (place - (1 - 2 * core) * step + self.chips) % self.chips
            if self.snake:
                owner = jnp.where(owner < half, 2 * owner, 2 * (self.chips - 1 - owner) + 1)
            names += [(step, True), (step, False), step]
            values += [2 * owner + core, 2 * owner + 1 - core, owner // key_share]
        values = lax.optimization_barrier([x.astype(jnp.int32) for x in values])
        self.numbers = dict(zip(names, values))
        return values

    def number(self, name):
        return self.numbers[name].reshape(1)

    def send(self, block, way):
        route = []
        for place in range(self.chips):
            for core in (0, 1):
                to = self.order[(place + (way if core == 0 else -way)) % self.chips]
                route.append((self.order[place] * 2 + core, to * 2 + core))
        return lax.ppermute(block, "ctx", sorted(route))

    def swap(self, block):
        return lax.ppermute(block, "ctx", [(i, i ^ 1) for i in range(2 * self.chips)])


def after(value, *others):
    return lax.optimization_barrier((value, *others))[0]


def near(x):
    return pltpu.with_memory_space_constraint(x, pltpu.VMEM)


def far(x):
    return pltpu.with_memory_space_constraint(x, pltpu.HBM)


def limit(megabytes):
    return pltpu.CompilerParams(vmem_limit_bytes=megabytes * 1024 * 1024)


def stat_rows(rows):
    return -(-3 * (rows // LANES) // TILE) * TILE


def diagonal():
    shape = (LANES, LANES)
    return lax.broadcasted_iota(jnp.int32, shape, 0) == lax.broadcasted_iota(jnp.int32, shape, 1)


def pack_stats(stats):
    high = [x.astype(BF16).astype(F32) for x in stats]
    rest = [x - h for x, h in zip(stats, high)]
    middle = [x.astype(BF16).astype(F32) for x in rest]
    low = [x - h for x, h in zip(rest, middle)]
    parts = high + middle + low
    parts += [jnp.zeros_like(stats[0])] * (-len(parts) % TILE)
    return jnp.concatenate(parts, axis=0).astype(BF16)


def unpack_stats(ref, rows):
    blocks = rows // LANES
    packed = ref[pl.ds(rows, stat_rows(rows)), :].astype(F32)
    return packed[:blocks] + packed[blocks : 2 * blocks] + packed[2 * blocks : 3 * blocks]


def fetch_columns(group, sources, targets, sems):
    columns = pl.ds(pl.multiple_of(group * LANES, LANES), LANES)
    tokens = sources[0].shape[0]
    copies = []
    for i, source in enumerate(sources):
        target = targets[i // 2].at[pl.ds((i % 2) * tokens, tokens), :]
        copies.append(pltpu.make_async_copy(source.at[:, columns], target, sems.at[i]))
        copies[-1].start()
    return copies


def prepare_kernel(this, pair, weight, last, weight_out, onehot, bias, sem):
    copy = pltpu.make_async_copy(weight, weight_out, sem)
    copy.start()
    shape = onehot.shape
    block = lax.broadcasted_iota(jnp.int32, shape, 0) // BLK
    lane = lax.broadcasted_iota(jnp.int32, shape, 1)
    onehot[...] = (block == lane).astype(F32).astype(BF16)
    blocks = shape[0] // BLK // 2
    lane = lax.broadcasted_iota(jnp.int32, bias.shape, 1)
    place = jnp.where(
        lane < blocks, this[0] * blocks + lane, (pair[0] - 1) * blocks + lane
    )
    bias[...] = jnp.where(place <= last[...], 0.0, MASKED).astype(BF16)
    copy.wait()


def prepare(ring, weight, last, tokens):
    queries = last.shape[0]
    return pl.pallas_call(
        prepare_kernel,
        out_shape=[
            pltpu.VMEM(weight.shape, BF16),
            pltpu.VMEM((tokens, LANES), BF16),
            pltpu.VMEM((queries, LANES), BF16),
        ],
        in_specs=[SCALARS, SCALARS, ANYWHERE, VMEM],
        out_specs=[VMEM] * 3,
        scratch_shapes=[pltpu.SemaphoreType.DMA],
        compiler_params=limit(8),
        cost_estimate=FREE,
        name="prepare",
    )(ring.number("self"), ring.number("pair"), far(weight), near(last))


def stage_kernel(source, target, sem):
    copy = pltpu.make_async_copy(source, target, sem)
    copy.start()
    copy.wait()


def stage(weight):
    return pl.pallas_call(
        stage_kernel,
        out_shape=pltpu.VMEM(weight.shape, weight.dtype),
        in_specs=[ANYWHERE],
        out_specs=VMEM,
        scratch_shapes=[pltpu.SemaphoreType.DMA],
        compiler_params=limit(8),
        cost_estimate=FREE,
        name="stage",
    )(far(weight))


def fetch_kernel(head, k0, k1, v0, v1, key, value, sems):
    for copy in fetch_columns(head[0], (k0, k1, v0, v1), (key, value), sems):
        copy.wait()


def fetch(head, cache):
    shape = pltpu.VMEM((2 * cache[0].shape[0], LANES), BF16)
    return pl.pallas_call(
        fetch_kernel,
        out_shape=[shape, shape],
        in_specs=[SCALARS] + [ANYWHERE] * 4,
        out_specs=[VMEM] * 2,
        scratch_shapes=[pltpu.SemaphoreType.DMA((4,))],
        compiler_params=limit(8),
        cost_estimate=FREE,
        name="fetch",
    )(head, far(cache[0]), cache[1], far(cache[2]), cache[3])


def attend_kernel(chunk, parts, following, q, bias, onehot, key, value, k0, k1, v0, v1, *refs):
    outs, (next_key, next_value, sems) = refs[:parts], refs[parts:]
    copies = fetch_columns(following[0], (k0, k1, v0, v1), (next_key, next_value), sems)
    rows = q.shape[0] // parts
    diag = diagonal()
    biases = jnp.concatenate([bias[...]] * (chunk // bias.shape[0]), axis=0)
    for part, out in enumerate(outs):
        stats = []
        for start in range(0, rows, chunk):
            query = jnp.concatenate(
                [q[pl.ds(part * rows + start, chunk), :], biases], axis=1
            )
            keys = jnp.concatenate([key[...], onehot[...]], axis=1)
            scores = lax.dot_general(
                query, keys, (((1,), (1,)), ((), ())), preferred_element_type=F32
            )
            peak = jnp.max(scores, axis=1, keepdims=True)
            weights = jnp.exp2(scores - peak).astype(BF16)
            values = jnp.concatenate([value[...], jnp.ones(value.shape, BF16)], axis=1)
            sums = jnp.dot(weights, values, preferred_element_type=F32)
            total = sums[:, LANES:]
            out[pl.ds(start, chunk), :] = (sums[:, :LANES] / total).astype(BF16)
            level = peak + jnp.log2(total)
            for b in range(chunk // LANES):
                block = level[b * LANES : (b + 1) * LANES]
                stats.append(jnp.sum(jnp.where(diag, block, 0.0), axis=0, keepdims=True))
        out[pl.ds(rows, stat_rows(rows)), :] = pack_stats(stats)
    for copy in copies:
        copy.wait()


def attend(following, q, parts, bias, onehot, head, cache):
    rows, width = q.shape[0] // parts, q.shape[1]
    chunk = math.gcd(rows, 256)
    shape = pltpu.VMEM(head[0].shape, BF16)
    out = pl.pallas_call(
        functools.partial(attend_kernel, chunk, parts),
        out_shape=[pltpu.VMEM((rows + stat_rows(rows), width), BF16)] * parts + [shape, shape],
        in_specs=[SCALARS] + [VMEM] * 5 + [ANYWHERE] * 4,
        out_specs=[VMEM] * (parts + 2),
        scratch_shapes=[pltpu.SemaphoreType.DMA((4,))],
        compiler_params=limit(16),
        cost_estimate=FREE,
        name="attend",
    )(following, *[near(x) for x in (q, bias, onehot, *head)], far(cache[0]), cache[1], far(cache[2]), cache[3])
    return out[:parts], out[parts:]


def spread(diag, row):
    high = row.astype(BF16).astype(F32)
    ones = jnp.ones((LANES, LANES), BF16)
    return sum(
        jnp.dot(jnp.where(diag, x, 0.0).astype(BF16), ones, preferred_element_type=F32)
        for x in (high, row - high)
    )


def merged(diag, block, one, one_stat, two, two_stat):
    peak = jnp.maximum(one_stat, two_stat)
    one_part, two_part = jnp.exp2(one_stat - peak), jnp.exp2(two_stat - peak)
    total = one_part + two_part
    share = spread(diag, one_part / total)
    here = pl.ds(block * LANES, LANES)
    one, two = one[here, :].astype(F32), two[here, :].astype(F32)
    return two + share * (one - two), peak + jnp.log2(total)


def merge_kernel(rows, one, two, out):
    diag = diagonal()
    one_stats, two_stats = unpack_stats(one, rows), unpack_stats(two, rows)
    stats = []
    for b in range(rows // LANES):
        value, stat = merged(diag, b, one, one_stats[b : b + 1], two, two_stats[b : b + 1])
        out[pl.ds(b * LANES, LANES), :] = value.astype(BF16)
        stats.append(stat)
    out[pl.ds(rows, stat_rows(rows)), :] = pack_stats(stats)


def merge(rows, one, two):
    return pl.pallas_call(
        functools.partial(merge_kernel, rows),
        out_shape=pltpu.VMEM(two.shape, BF16),
        in_specs=[VMEM, VMEM],
        out_specs=VMEM,
        cost_estimate=FREE,
        compiler_params=limit(8),
        name="merge",
    )(near(one), near(two))


def finish_kernel(rows, queries, *refs):
    diag = diagonal()
    for half in range(2):
        parts, out = refs[3 * half : 3 * half + 3], refs[6 + half]
        width = parts[0].shape[1]
        stats = [unpack_stats(part, rows) for part in parts]
        for b in range(rows // LANES):
            here = pl.ds(b * LANES, LANES)
            levels = [stat[b : b + 1] for stat in stats]
            peak = functools.reduce(jnp.maximum, levels)
            shares = [jnp.exp2(level - peak) for level in levels]
            total = sum(shares)
            value = sum(
                spread(diag, share / total) * part[here, :].astype(F32)
                for share, part in zip(shares, parts)
            ).astype(BF16)
            for piece in range(LANES // queries):
                head = (b * LANES) // queries + piece
                out[:, pl.ds(head * width, width)] = value[piece * queries : (piece + 1) * queries]


def finish(rows, queries, own, other):
    width = own[0].shape[1]
    shape = pltpu.VMEM((queries, rows // queries * width), BF16)
    return pl.pallas_call(
        functools.partial(finish_kernel, rows, queries),
        out_shape=[shape, shape],
        in_specs=[VMEM] * 6,
        out_specs=[VMEM] * 2,
        cost_estimate=FREE,
        compiler_params=limit(8),
        name="finish",
    )(*[near(x) for x in (*own, *other)])


def head_norm_kernel(features, scale, sums, squares, gain, out):
    queries = sums.shape[0]
    width = gain.shape[1]
    factor = lax.rsqrt(jnp.sum(squares[...], axis=1, keepdims=True) / features + EPSILON)
    gains = gain[...].astype(F32) * scale
    for head in range(sums.shape[1] // width):
        value = sums[:, pl.ds(head * width, width)] * factor
        mean = jnp.mean(value * value, axis=1, keepdims=True)
        out[pl.ds(head * queries, queries), :] = (
            value * lax.rsqrt(mean + EPSILON) * gains
        ).astype(BF16)


def head_norm(sums, squares, gain, features):
    queries, width = sums.shape[0], gain.shape[0]
    heads = sums.shape[1] // width
    return pl.pallas_call(
        functools.partial(head_norm_kernel, features, width**-0.5 * math.log2(math.e)),
        out_shape=pltpu.VMEM((heads * queries, width), BF16),
        in_specs=[VMEM] * 3,
        out_specs=VMEM,
        cost_estimate=FREE,
        compiler_params=limit(8),
        name="head_norm",
    )(near(sums), near(squares), near(gain[None, :]))


def project_kernel(count, queries, carried, begun, *refs):
    blocks, parts = refs[:count], refs[count : 2 * count]
    gains, row = (parts, queries) if carried else (refs[2 * count : 3 * count], queries + 1)
    rest = refs[(2 if carried else 3) * count :]
    weight, state, (sums, squares) = rest[0], rest[1:-2], rest[-2:]
    total, square = (state[0][...], state[1][...]) if begun else (0.0, 0.0)
    for block, part, gain in zip(blocks, parts, gains):
        width = part.shape[1]
        values = part[...][:queries].astype(F32)
        scaled = (values * gain[...][row : row + 1].astype(F32)).astype(BF16)
        piece = weight[pl.ds(pl.multiple_of(block[0] * width, width), width), :]
        total += jnp.dot(scaled, piece, preferred_element_type=F32)
        for lane in range(0, width, LANES):
            square += values[:, lane : lane + LANES] * values[:, lane : lane + LANES]
    sums[...] = total
    squares[...] = square


def project(queries, blocks, parts, gains, weight, state):
    arrays = [*parts, *(gains or ()), weight, *(state or ())]
    return pl.pallas_call(
        functools.partial(project_kernel, len(parts), queries, not gains, bool(state)),
        out_shape=[
            pltpu.VMEM((queries, weight.shape[1]), F32),
            pltpu.VMEM((queries, LANES), F32),
        ],
        in_specs=[SCALARS] * len(blocks) + [VMEM] * len(arrays),
        out_specs=[VMEM] * 2,
        compiler_params=limit(8),
        cost_estimate=FREE,
        name="project",
    )(*blocks, *[near(x) for x in arrays])


def gather_project(ring, queries, own, other, carriers, weight, beside=()):
    arrived, waiting, state = {}, [], None
    for step in range(ring.rounds + 1):
        last = step == ring.rounds
        parts = [(step, True, own)] + ([] if last else [(step, False, other)])
        if not last:
            own = ring.send(own if state is None else after(own, state[0]), 1)
        if step < ring.rounds - 1:
            other = ring.send(other, 1)
        if step > 0:
            for _, mine, part in list(parts):
                opposite = ring.swap(part)
                if step == 1 and mine and beside:
                    opposite, *beside[:] = lax.optimization_barrier((opposite, *beside))
                parts.append((-step, not mine, opposite))
        for at, mine, part in parts:
            arrived[at, mine] = part
            waiting.append((at, mine))
        if last or step % 3 == 2:
            state = project(
                queries,
                [ring.number(name) for name in waiting],
                [arrived[name] for name in waiting],
                carriers and [carriers[name] for name in waiting],
                weight,
                state,
            )
            waiting = []
    return state[0], state[1], arrived


def mix_kernel(count, *refs):
    blocks, (one, two, one_weight, two_weight) = refs[:count], refs[count : count + 4]
    outs, (pieces, sems) = refs[count + 4 : -2], refs[-2:]
    width = outs[0].shape[1]
    copies = []
    for i, block in enumerate(blocks):
        columns = pl.ds(pl.multiple_of(block[0] * width, width), width)
        for j, weight in enumerate((one_weight, two_weight)):
            copies.append(
                pltpu.make_async_copy(weight.at[:, columns], pieces.at[i, j], sems.at[i, j])
            )
            copies[-1].start()
    for i, out in enumerate(outs):
        value = 0.0
        for j, rows in enumerate((one, two)):
            copies[2 * i + j].wait()
            value += jnp.dot(rows[...], pieces[i, j], preferred_element_type=F32)
        out[...] = value.astype(out.dtype)


def mix(blocks, width, kind, one, two, one_weight, two_weight):
    queries, depth = one.shape
    return pl.pallas_call(
        functools.partial(mix_kernel, len(blocks)),
        out_shape=[pltpu.VMEM((queries, width), kind)] * len(blocks),
        in_specs=[SCALARS] * len(blocks) + [VMEM, VMEM, ANYWHERE, ANYWHERE],
        out_specs=[VMEM] * len(blocks),
        scratch_shapes=[
            pltpu.VMEM((len(blocks), 2, depth, width), BF16),
            pltpu.SemaphoreType.DMA((len(blocks), 2)),
        ],
        compiler_params=limit(16),
        cost_estimate=FREE,
        name="mix",
    )(*blocks, near(one), near(two), far(one_weight), two_weight)


def add_kernel(*refs):
    rows = refs[-1].shape[0]
    refs[-1][...] = sum(ref[...][:rows].astype(F32) for ref in refs[:-1]).astype(BF16)


def add(*parts):
    return pl.pallas_call(
        add_kernel,
        out_shape=pltpu.VMEM(parts[0].shape, BF16),
        in_specs=[VMEM] * len(parts),
        out_specs=VMEM,
        compiler_params=limit(8),
        cost_estimate=FREE,
        name="add",
    )(*[near(x) for x in parts])


def join_kernel(one, two, out):
    rows = one.shape[0]
    out[:rows] = one[...]
    out[rows:] = two[...]


def join(one, two):
    return pl.pallas_call(
        join_kernel,
        out_shape=pltpu.VMEM((2 * one.shape[0], one.shape[1]), one.dtype),
        in_specs=[VMEM, VMEM],
        out_specs=VMEM,
        compiler_params=limit(8),
        cost_estimate=FREE,
        name="join",
    )(near(one), near(two))


def first_half_kernel(both, out):
    out[...] = both[: out.shape[0]]


def first_half(both):
    return pl.pallas_call(
        first_half_kernel,
        out_shape=pltpu.VMEM((both.shape[0] // 2, both.shape[1]), both.dtype),
        in_specs=[VMEM],
        out_specs=VMEM,
        compiler_params=limit(8),
        cost_estimate=FREE,
        name="first_half",
    )(near(both))


def on_device(
    columns,
    hidden,
    attn_gain,
    q_weight,
    q_gain,
    key_cache,
    value_cache,
    block_limit,
    out_weight,
    next_gain,
    next_weight,
):
    ring = Ring(lax.axis_size("ctx"), columns)
    rounds = ring.rounds
    queries, here = hidden.shape
    features = q_weight.shape[0]
    head_dim = q_gain.shape[0]
    heads_here = q_weight.shape[1] // head_dim
    rows = heads_here * queries
    kv_heads = key_cache.shape[1] // head_dim
    group_size = heads_here * 2 * ring.chips // kv_heads

    numbers = ring.locate(group_size // (2 * heads_here))

    row = jnp.arange(queries + 2, dtype=jnp.int32)[:, None]
    own = jnp.where(
        row < queries,
        jnp.pad(hidden, ((0, 2), (0, 0))),
        jnp.where(row == queries, attn_gain[None, :], next_gain[None, :]),
    )
    last = jnp.broadcast_to(block_limit[:, None], (queries, LANES))
    own, last = after(own, *numbers), after(last, *numbers)
    other, other_keys = lax.optimization_barrier((ring.swap(own), ring.swap(key_cache)))
    beside = [ring.swap(value_cache)]
    near_weight, onehot, bias = prepare(ring, q_weight, last, 2 * key_cache.shape[0])
    sums, squares, carriers = gather_project(
        ring, queries, own, other, None, near_weight, beside
    )
    cache = (key_cache, other_keys, value_cache, *beside)
    own_heads = head_norm(sums, squares, q_gain, features)
    travelling = join(own_heads, ring.swap(own_heads))
    other_weight = ring.swap(after(out_weight, travelling))

    partials = []
    done = own_heads
    head = fetch(ring.number(0), cache)
    for step in range(rounds + 1):
        if step < rounds:
            block = travelling if step < rounds - 1 else first_half(travelling)
            coming = ring.send(after(block, done), 1)
        following = ring.number(min(step + 1, rounds))
        if step == 0:
            parts, head = attend(following, own_heads, 1, bias, onehot, head, cache)
            local_other = ring.swap(parts[0])
        else:
            count = 2 if step < rounds else 1
            parts, head = attend(following, travelling, count, bias, onehot, head, cache)
        partials.append(parts)
        done = parts[0]
        travelling = coming
    own = ring.send(partials[rounds][0], -1)
    other = ring.send(partials[rounds - 1][1], -1)
    for step in range(rounds - 1, 0, -1):
        own = ring.send(merge(rows, own, partials[step][0]), -1)
        if step > 1:
            other = ring.send(merge(rows, other, partials[step - 1][1]), -1)
    own_far, other_far = ring.swap(own), ring.swap(other)
    attended, attended_other = finish(
        rows, queries, (own, other_far, partials[0][0]), (other, own_far, local_other)
    )

    def mixed(kind, places):
        blocks = [ring.number(place) for place in places]
        weights = (out_weight, other_weight)
        parts = mix(blocks, here, kind, attended, attended_other, *weights)
        return dict(zip(places, parts))

    first = [(rounds, True), (rounds - 1, False)]
    places = [(step, mine) for step in range(rounds - 1, -1, -1) for mine in (True, False)]
    shares = mixed(BF16, first)
    own, other = (ring.send(shares[place], -1) for place in first)
    shares = mixed(F32, [place for place in places if place not in first])
    near_weight = stage(after(next_weight, shares[0, True]))
    for step in range(rounds - 1, 0, -1):
        if step == rounds - 2:
            own, near_weight = lax.optimization_barrier((own, near_weight))
        own = ring.send(add(shares[step, True], own), -1)
        if step > 1:
            other = ring.send(add(shares[step - 1, False], other), -1)
    own_far, other_far = ring.swap(own), ring.swap(other)
    new_own = add(shares[0, True], own, other_far, carriers[0, True])
    new_other = add(shares[0, False], other, own_far, carriers[0, False])

    sums, squares, _ = gather_project(
        ring, queries, new_own, new_other, carriers, near_weight
    )
    factor = lax.rsqrt(jnp.sum(squares, axis=1, keepdims=True) / features + EPSILON)
    return new_own, (sums * factor).astype(BF16)


def solution(mesh):
    in_specs = (
        P("groups", "ctx"),
        P("ctx"),
        P(None, "ctx"),
        P(),
        P(("groups", "ctx"), None),
        P(("groups", "ctx"), None),
        P("groups"),
        P("ctx", None),
        P("ctx"),
        P(None, "ctx"),
    )
    out_specs = (P("groups", "ctx"), P("groups", "ctx"))
    columns = 2 if mesh.shape["groups"] == 2 else 1
    return jax.shard_map(
        functools.partial(on_device, columns),
        mesh=mesh,
        in_specs=in_specs,
        out_specs=out_specs,
        check_vma=False,
    )
```

```python
import functools
import math

import jax
import jax.numpy as jnp
from jax import lax
from jax.experimental import pallas as pl
from jax.experimental.pallas import tpu as pltpu
from jax.sharding import PartitionSpec as P

BLK = 128
EPSILON = 1e-05
MASKED = -1e30
LANES = 128
TILE = 16
BF16 = jnp.bfloat16
F32 = jnp.float32
VMEM = pl.BlockSpec(memory_space=pltpu.VMEM)
ANYWHERE = pl.BlockSpec(memory_space=pl.ANY)
SCALARS = pl.BlockSpec(memory_space=pltpu.SMEM)


FREE = pl.CostEstimate(flops=0, bytes_accessed=0, transcendentals=0)


class Ring:
    def __init__(self, devices, columns):
        self.chips = devices // 2
        self.rounds = self.chips // 2
        self.snake = columns == 2 and self.chips % 2 == 0
        if self.snake:
            self.order = list(range(0, self.chips, 2)) + list(range(1, self.chips, 2))[::-1]
        else:
            self.order = list(range(self.chips))

    def locate(self, key_share):
        device = lax.axis_index("ctx")
        core, chip = device % 2, device // 2
        middle = self.chips // 2
        if self.snake:
            place = jnp.where(chip % 2 == 0, chip // 2, self.chips - 1 - chip // 2)
        else:
            place = chip
        sign = 1 - 2 * ((core + place) % 2)
        names, values = ["self", "pair"], [device, device + 1 - 2 * core]
        for step in range(-self.rounds, self.rounds + 1):
            owner = (place - sign * step + self.chips) % self.chips
            if self.snake:
                owner = jnp.where(owner < middle, 2 * owner, 2 * (self.chips - 1 - owner) + 1)
            names += [(step, True), (step, False), step]
            half = core if step % 2 == 0 else 1 - core
            values += [2 * owner + half, 2 * owner + 1 - half, owner // key_share]
        values = lax.optimization_barrier([x.astype(jnp.int32) for x in values])
        self.numbers = dict(zip(names, values))
        return values

    def number(self, name):
        return self.numbers[name].reshape(1)

    def send(self, block, way):
        route = []
        for place in range(self.chips):
            for core in (0, 1):
                ahead = way if (core + place) % 2 == 0 else -way
                to = self.order[(place + ahead) % self.chips]
                route.append((self.order[place] * 2 + core, to * 2 + 1 - core))
        return lax.ppermute(block, "ctx", sorted(route))

    def swap(self, block):
        return lax.ppermute(block, "ctx", [(i, i ^ 1) for i in range(2 * self.chips)])


def after(value, *others):
    return lax.optimization_barrier((value, *others))[0]


def near(x):
    return pltpu.with_memory_space_constraint(x, pltpu.VMEM)


def far(x):
    return pltpu.with_memory_space_constraint(x, pltpu.HBM)


def limit(megabytes):
    return pltpu.CompilerParams(vmem_limit_bytes=megabytes * 1024 * 1024)


def stat_rows(rows):
    return -(-3 * (rows // LANES) // TILE) * TILE


def diagonal():
    shape = (LANES, LANES)
    return lax.broadcasted_iota(jnp.int32, shape, 0) == lax.broadcasted_iota(jnp.int32, shape, 1)


def pack_stats(stats):
    high = [x.astype(BF16).astype(F32) for x in stats]
    rest = [x - h for x, h in zip(stats, high)]
    middle = [x.astype(BF16).astype(F32) for x in rest]
    low = [x - h for x, h in zip(rest, middle)]
    parts = high + middle + low
    parts += [jnp.zeros_like(stats[0])] * (-len(parts) % TILE)
    return jnp.concatenate(parts, axis=0).astype(BF16)


def unpack_stats(ref, rows):
    blocks = rows // LANES
    packed = ref[pl.ds(rows, stat_rows(rows)), :].astype(F32)
    return packed[:blocks] + packed[blocks : 2 * blocks] + packed[2 * blocks : 3 * blocks]


def fetch_columns(group, sources, targets, sems):
    columns = pl.ds(pl.multiple_of(group * LANES, LANES), LANES)
    tokens = sources[0].shape[0]
    copies = []
    for i, source in enumerate(sources):
        target = targets[i // 2].at[pl.ds((i % 2) * tokens, tokens), :]
        copies.append(pltpu.make_async_copy(source.at[:, columns], target, sems.at[i]))
        copies[-1].start()
    return copies


def prepare_kernel(this, pair, last, onehot, bias):
    shape = onehot.shape
    block = lax.broadcasted_iota(jnp.int32, shape, 0) // BLK
    lane = lax.broadcasted_iota(jnp.int32, shape, 1)
    onehot[...] = (block == lane).astype(F32).astype(BF16)
    blocks = shape[0] // BLK // 2
    lane = lax.broadcasted_iota(jnp.int32, bias.shape, 1)
    place = jnp.where(
        lane < blocks, this[0] * blocks + lane, (pair[0] - 1) * blocks + lane
    )
    bias[...] = jnp.where(place <= last[...], 0.0, MASKED).astype(BF16)


def prepare(ring, last, tokens):
    queries = last.shape[0]
    return pl.pallas_call(
        prepare_kernel,
        out_shape=[
            pltpu.VMEM((tokens, LANES), BF16),
            pltpu.VMEM((queries, LANES), BF16),
        ],
        in_specs=[SCALARS, SCALARS, VMEM],
        out_specs=[VMEM] * 2,
        compiler_params=limit(8),
        cost_estimate=FREE,
        name="prepare",
    )(ring.number("self"), ring.number("pair"), near(last))


def stage_kernel(source, target, sem):
    copy = pltpu.make_async_copy(source, target, sem)
    copy.start()
    copy.wait()


def stage(weight):
    return pl.pallas_call(
        stage_kernel,
        out_shape=pltpu.VMEM(weight.shape, weight.dtype),
        in_specs=[ANYWHERE],
        out_specs=VMEM,
        scratch_shapes=[pltpu.SemaphoreType.DMA],
        compiler_params=limit(8),
        cost_estimate=FREE,
        name="stage",
    )(far(weight))


def fetch_kernel(head, k0, k1, v0, v1, key, value, sems):
    for copy in fetch_columns(head[0], (k0, k1, v0, v1), (key, value), sems):
        copy.wait()


def fetch(head, cache):
    shape = pltpu.VMEM((2 * cache[0].shape[0], LANES), BF16)
    return pl.pallas_call(
        fetch_kernel,
        out_shape=[shape, shape],
        in_specs=[SCALARS] + [ANYWHERE] * 4,
        out_specs=[VMEM] * 2,
        scratch_shapes=[pltpu.SemaphoreType.DMA((4,))],
        compiler_params=limit(8),
        cost_estimate=FREE,
        name="fetch",
    )(head, far(cache[0]), cache[1], far(cache[2]), cache[3])


def attend_kernel(chunk, parts, q, bias, onehot, key, value, *refs):
    copies = []
    if len(refs) > parts:
        following, *cache = refs[:5]
        outs, (next_key, next_value, sems) = refs[5 : 5 + parts], refs[5 + parts :]
        copies = fetch_columns(following[0], cache, (next_key, next_value), sems)
    else:
        outs = refs
    rows = q.shape[0] // parts
    diag = diagonal()
    biases = jnp.concatenate([bias[...]] * (chunk // bias.shape[0]), axis=0)
    for part, out in enumerate(outs):
        stats = []
        for start in range(0, rows, chunk):
            query = jnp.concatenate(
                [q[pl.ds(part * rows + start, chunk), :], biases], axis=1
            )
            keys = jnp.concatenate([key[...], onehot[...]], axis=1)
            scores = lax.dot_general(
                query, keys, (((1,), (1,)), ((), ())), preferred_element_type=F32
            )
            peak = jnp.max(scores, axis=1, keepdims=True)
            weights = jnp.exp2(scores - peak).astype(BF16)
            values = jnp.concatenate([value[...], jnp.ones(value.shape, BF16)], axis=1)
            sums = jnp.dot(weights, values, preferred_element_type=F32)
            total = sums[:, LANES:]
            out[pl.ds(start, chunk), :] = (sums[:, :LANES] / total).astype(BF16)
            level = peak + jnp.log2(total)
            for b in range(chunk // LANES):
                block = level[b * LANES : (b + 1) * LANES]
                stats.append(jnp.sum(jnp.where(diag, block, 0.0), axis=0, keepdims=True))
        out[pl.ds(rows, stat_rows(rows)), :] = pack_stats(stats)
    for copy in copies:
        copy.wait()


def attend(following, q, parts, bias, onehot, head, cache):
    rows, width = q.shape[0] // parts, q.shape[1]
    chunk = math.gcd(rows, 256)
    shapes = [pltpu.VMEM((rows + stat_rows(rows), width), BF16)] * parts
    arrays = [near(x) for x in (q, bias, onehot, *head)]
    specs, scratch = [VMEM] * 5, []
    if following is not None:
        shapes += [pltpu.VMEM(head[0].shape, BF16)] * 2
        arrays += [following, far(cache[0]), cache[1], far(cache[2]), cache[3]]
        specs += [SCALARS] + [ANYWHERE] * 4
        scratch = [pltpu.SemaphoreType.DMA((4,))]
    out = pl.pallas_call(
        functools.partial(attend_kernel, chunk, parts),
        out_shape=shapes,
        in_specs=specs,
        out_specs=[VMEM] * len(shapes),
        scratch_shapes=scratch,
        compiler_params=limit(16),
        cost_estimate=FREE,
        name="attend",
    )(*arrays)
    return out[:parts], out[parts:]


def spread(diag, row):
    high = row.astype(BF16).astype(F32)
    ones = jnp.ones((LANES, LANES), BF16)
    return sum(
        jnp.dot(jnp.where(diag, x, 0.0).astype(BF16), ones, preferred_element_type=F32)
        for x in (high, row - high)
    )


def merged(diag, block, one, one_stat, two, two_stat):
    peak = jnp.maximum(one_stat, two_stat)
    one_part, two_part = jnp.exp2(one_stat - peak), jnp.exp2(two_stat - peak)
    total = one_part + two_part
    share = spread(diag, one_part / total)
    here = pl.ds(block * LANES, LANES)
    one, two = one[here, :].astype(F32), two[here, :].astype(F32)
    return two + share * (one - two), peak + jnp.log2(total)


def merge_kernel(rows, one, two, out):
    diag = diagonal()
    one_stats, two_stats = unpack_stats(one, rows), unpack_stats(two, rows)
    stats = []
    for b in range(rows // LANES):
        value, stat = merged(diag, b, one, one_stats[b : b + 1], two, two_stats[b : b + 1])
        out[pl.ds(b * LANES, LANES), :] = value.astype(BF16)
        stats.append(stat)
    out[pl.ds(rows, stat_rows(rows)), :] = pack_stats(stats)


def merge(rows, one, two):
    return pl.pallas_call(
        functools.partial(merge_kernel, rows),
        out_shape=pltpu.VMEM(two.shape, BF16),
        in_specs=[VMEM, VMEM],
        out_specs=VMEM,
        cost_estimate=FREE,
        compiler_params=limit(8),
        name="merge",
    )(near(one), near(two))


def finish_kernel(rows, queries, *refs):
    diag = diagonal()
    for half in range(2):
        parts, out = refs[3 * half : 3 * half + 3], refs[6 + half]
        width = parts[0].shape[1]
        stats = [unpack_stats(part, rows) for part in parts]
        for b in range(rows // LANES):
            here = pl.ds(b * LANES, LANES)
            levels = [stat[b : b + 1] for stat in stats]
            peak = functools.reduce(jnp.maximum, levels)
            shares = [jnp.exp2(level - peak) for level in levels]
            total = sum(shares)
            value = sum(
                spread(diag, share / total) * part[here, :].astype(F32)
                for share, part in zip(shares, parts)
            ).astype(BF16)
            for piece in range(LANES // queries):
                head = (b * LANES) // queries + piece
                out[:, pl.ds(head * width, width)] = value[piece * queries : (piece + 1) * queries]


def finish(rows, queries, own, other):
    width = own[0].shape[1]
    shape = pltpu.VMEM((queries, rows // queries * width), BF16)
    return pl.pallas_call(
        functools.partial(finish_kernel, rows, queries),
        out_shape=[shape, shape],
        in_specs=[VMEM] * 6,
        out_specs=[VMEM] * 2,
        cost_estimate=FREE,
        compiler_params=limit(8),
        name="finish",
    )(*[near(x) for x in (*own, *other)])


def project_kernel(count, queries, features, scale, carried, begun, *refs):
    blocks, parts = refs[:count], refs[count : 2 * count]
    gains, row = (parts, queries) if carried else (refs[2 * count : 3 * count], queries + 1)
    weight, *rest = refs[(2 if carried else 3) * count :]
    total, square = 0.0, 0.0
    if begun:
        total, square = rest[0][...], rest[1][...]
    rest = rest[2 if begun else 0 :]
    for block, part, gain in zip(blocks, parts, gains):
        width = part.shape[1]
        values = part[...][:queries].astype(F32)
        scaled = (values * gain[...][row : row + 1].astype(F32)).astype(BF16)
        piece = weight[pl.ds(pl.multiple_of(block[0] * width, width), width), :]
        total += jnp.dot(scaled, piece, preferred_element_type=F32)
        for lane in range(0, width, LANES):
            square += values[:, lane : lane + LANES] * values[:, lane : lane + LANES]
    if not features:
        rest[0][...] = total
        rest[1][...] = square
        return
    factor = lax.rsqrt(jnp.sum(square, axis=1, keepdims=True) / features + EPSILON)
    if scale is None:
        rest[0][...] = (total * factor).astype(BF16)
        return
    gain, out = rest
    width = gain.shape[1]
    for head in range(total.shape[1] // width):
        value = total[:, head * width : (head + 1) * width] * factor
        mean = jnp.mean(value * value, axis=1, keepdims=True)
        out[pl.ds(head * queries, queries), :] = (
            value * lax.rsqrt(mean + EPSILON) * (gain[...].astype(F32) * scale)
        ).astype(BF16)


def project(queries, blocks, parts, gains, weight, state, last=False, head_gain=None):
    arrays = [*parts, *(gains or ()), weight, *(state or ())]
    width, scale = weight.shape[1], None
    shapes = [pltpu.VMEM((queries, width), F32), pltpu.VMEM((queries, LANES), F32)]
    if head_gain is not None:
        arrays.append(head_gain[None, :])
        depth = head_gain.shape[0]
        scale = depth**-0.5 * math.log2(math.e)
        shapes = [pltpu.VMEM((width // depth * queries, depth), BF16)]
    elif last:
        shapes = [jax.ShapeDtypeStruct((queries, width), BF16)]
    features = weight.shape[0] if last else 0
    return pl.pallas_call(
        functools.partial(
            project_kernel, len(parts), queries, features, scale, not gains, bool(state)
        ),
        out_shape=shapes,
        in_specs=[SCALARS] * len(blocks) + [VMEM] * len(arrays),
        out_specs=[VMEM] * len(shapes),
        compiler_params=limit(8),
        cost_estimate=FREE,
        name="project",
    )(*blocks, *[near(x) for x in arrays])


def gather_project(ring, queries, own, other, carriers, weight, beside=None, head_gain=None):
    arrived, waiting, swapped, state = {}, [], [], None

    def flush(names, state, **how):
        return project(
            queries,
            [ring.number(name) for name in names],
            [arrived[name] for name in names],
            carriers and [carriers[name] for name in names],
            weight,
            state,
            **how,
        )

    for step in range(ring.rounds + 1):
        halves = (True, False) if step < ring.rounds else (True,)
        for mine, part in zip(halves, (own, other)):
            arrived[step, mine] = part
            waiting.append((step, mine))
        if step < ring.rounds:
            own = after(own, *(beside or {}).get(step + 1, ()), *(state or ()))
            own = ring.send(own, 1)
        if step < ring.rounds - 1:
            other = ring.send(other, 1)
        for mine in halves if step else ():
            arrived[-step, not mine] = ring.swap(arrived[step, mine])
            swapped.append((-step, not mine))
        if carriers and step % 3 == 2 and step < ring.rounds:
            state, waiting = flush(waiting, state), []
    (result,) = flush(waiting + swapped, state, last=True, head_gain=head_gain)
    return result, arrived


def mix_kernel(count, *refs):
    blocks, (one, two, one_weight, two_weight) = refs[:count], refs[count : count + 4]
    for block, out in zip(blocks, refs[count + 4 :]):
        width = out.shape[1]
        columns = pl.ds(pl.multiple_of(block[0] * width, width), width)
        value = jnp.dot(one[...], one_weight[:, columns], preferred_element_type=F32)
        value += jnp.dot(two[...], two_weight[:, columns], preferred_element_type=F32)
        out[...] = value.astype(out.dtype)


def mix(blocks, width, kind, one, two, one_weight, two_weight):
    return pl.pallas_call(
        functools.partial(mix_kernel, len(blocks)),
        out_shape=[pltpu.VMEM((one.shape[0], width), kind)] * len(blocks),
        in_specs=[SCALARS] * len(blocks) + [VMEM] * 4,
        out_specs=[VMEM] * len(blocks),
        compiler_params=limit(8),
        cost_estimate=FREE,
        name="mix",
    )(*blocks, *[near(x) for x in (one, two, one_weight, two_weight)])


def add_kernel(*refs):
    rows = refs[-1].shape[0]
    refs[-1][...] = sum(ref[...][:rows].astype(F32) for ref in refs[:-1]).astype(BF16)


def add(*parts):
    return pl.pallas_call(
        add_kernel,
        out_shape=pltpu.VMEM(parts[0].shape, BF16),
        in_specs=[VMEM] * len(parts),
        out_specs=VMEM,
        compiler_params=limit(8),
        cost_estimate=FREE,
        name="add",
    )(*[near(x) for x in parts])


def join_kernel(one, two, out):
    rows = one.shape[0]
    out[:rows] = one[...]
    out[rows:] = two[...]


def join(one, two):
    return pl.pallas_call(
        join_kernel,
        out_shape=pltpu.VMEM((2 * one.shape[0], one.shape[1]), one.dtype),
        in_specs=[VMEM, VMEM],
        out_specs=VMEM,
        compiler_params=limit(8),
        cost_estimate=FREE,
        name="join",
    )(near(one), near(two))


def first_half_kernel(both, out):
    out[...] = both[: out.shape[0]]


def first_half(both):
    return pl.pallas_call(
        first_half_kernel,
        out_shape=pltpu.VMEM((both.shape[0] // 2, both.shape[1]), both.dtype),
        in_specs=[VMEM],
        out_specs=VMEM,
        compiler_params=limit(8),
        cost_estimate=FREE,
        name="first_half",
    )(near(both))


def on_device(
    columns,
    hidden,
    attn_gain,
    q_weight,
    q_gain,
    key_cache,
    value_cache,
    block_limit,
    out_weight,
    next_gain,
    next_weight,
):
    ring = Ring(lax.axis_size("ctx"), columns)
    rounds = ring.rounds
    queries, here = hidden.shape
    head_dim = q_gain.shape[0]
    heads_here = q_weight.shape[1] // head_dim
    rows = heads_here * queries
    kv_heads = key_cache.shape[1] // head_dim
    group_size = heads_here * 2 * ring.chips // kv_heads

    numbers = ring.locate(group_size // (2 * heads_here))

    row = jnp.arange(queries + 2, dtype=jnp.int32)[:, None]
    own = jnp.where(
        row < queries,
        jnp.pad(hidden, ((0, 2), (0, 0))),
        jnp.where(row == queries, attn_gain[None, :], next_gain[None, :]),
    )
    last = jnp.broadcast_to(block_limit[:, None], (queries, LANES))
    own, last = after(own, *numbers), after(last, *numbers)
    other = ring.swap(own)
    other_keys = ring.swap(after(key_cache, other))
    other_values = ring.swap(after(value_cache, other))
    cache = (key_cache, other_keys, value_cache, other_values)
    onehot, bias = prepare(ring, last, 2 * key_cache.shape[0])
    head = fetch(ring.number(0), cache)
    beside = {rounds - 1: (other_keys,), rounds: (*head, bias)}
    own_heads, carriers = gather_project(
        ring, queries, own, other, None, q_weight, beside, q_gain
    )
    other_heads = ring.swap(own_heads)
    other_weight = ring.swap(after(out_weight, other_heads))

    partials = []
    done = own_heads
    for step in range(rounds + 1):
        if step == 0:
            coming = join(ring.send(own_heads, 1), ring.send(other_heads, 1))
        elif step < rounds:
            block = travelling if step < rounds - 1 else first_half(travelling)
            coming = ring.send(after(block, done), 1)
        following = ring.number(step + 1) if step < rounds else None
        if step == 0:
            parts, head = attend(following, own_heads, 1, bias, onehot, head, cache)
            local_other = ring.swap(parts[0])
        else:
            count = 2 if step < rounds else 1
            parts, head = attend(following, travelling, count, bias, onehot, head, cache)
        partials.append(parts)
        done = parts[0]
        travelling = coming
    own = ring.send(partials[rounds][0], -1)
    other = ring.send(partials[rounds - 1][1], -1)
    for step in range(rounds - 1, 0, -1):
        own = ring.send(merge(rows, own, partials[step][0]), -1)
        if step > 1:
            other = ring.send(merge(rows, other, partials[step - 1][1]), -1)
    own_far, other_far = ring.swap(own), ring.swap(other)
    attended, attended_other = finish(
        rows, queries, (own, other_far, partials[0][0]), (other, own_far, local_other)
    )

    def mixed(kind, places):
        blocks = [ring.number(place) for place in places]
        weights = (out_weight, other_weight)
        parts = mix(blocks, here, kind, attended, attended_other, *weights)
        return dict(zip(places, parts))

    first = [(rounds, True), (rounds - 1, False)]
    places = [(step, mine) for step in range(rounds - 1, -1, -1) for mine in (True, False)]
    shares = mixed(BF16, first) | mixed(F32, [place for place in places if place not in first])
    own, other = (ring.send(shares[place], -1) for place in first)
    for step in range(rounds - 1, 0, -1):
        own = ring.send(add(shares[step, True], own), -1)
        if step > 1:
            other = ring.send(add(shares[step - 1, False], other), -1)
    own_far, other_far = ring.swap(own), ring.swap(other)
    new_own = add(shares[0, True], own, other_far, carriers[0, True])
    new_other = add(shares[0, False], other, own_far, carriers[0, False])
    next_queries, _ = gather_project(ring, queries, new_own, new_other, carriers, next_weight)
    return new_own, next_queries


def solution(mesh):
    in_specs = (
        P("groups", "ctx"),
        P("ctx"),
        P(None, "ctx"),
        P(),
        P(("groups", "ctx"), None),
        P(("groups", "ctx"), None),
        P("groups"),
        P("ctx", None),
        P("ctx"),
        P(None, "ctx"),
    )
    out_specs = (P("groups", "ctx"), P("groups", "ctx"))
    columns = 2 if mesh.shape["groups"] == 2 else 1
    return jax.shard_map(
        functools.partial(on_device, columns),
        mesh=mesh,
        in_specs=in_specs,
        out_specs=out_specs,
        check_vma=False,
    )
```

```python
import functools
import math

import jax
import jax.numpy as jnp
from jax import lax
from jax.experimental import pallas as pl
from jax.experimental.pallas import tpu as pltpu
from jax.sharding import PartitionSpec as P

BLK = 128
EPSILON = 1e-05
MASKED = -1e30
LANES = 128
TILE = 16
BF16 = jnp.bfloat16
F32 = jnp.float32
VMEM = pl.BlockSpec(memory_space=pltpu.VMEM)
ANYWHERE = pl.BlockSpec(memory_space=pl.ANY)
SCALARS = pl.BlockSpec(memory_space=pltpu.SMEM)


FREE = pl.CostEstimate(flops=0, bytes_accessed=0, transcendentals=0)


def took(microseconds):
    return pl.CostEstimate(
        flops=int(microseconds * 1.15e9), bytes_accessed=0, transcendentals=0
    )


class Ring:
    def __init__(self, devices, columns):
        self.chips = devices // 2
        self.rounds = self.chips // 2
        self.snake = columns == 2 and self.chips % 2 == 0
        if self.snake:
            self.order = list(range(0, self.chips, 2)) + list(range(1, self.chips, 2))[::-1]
        else:
            self.order = list(range(self.chips))

    def locate(self, key_share):
        device = lax.axis_index("ctx")
        two = jnp.int32(2)
        core, chip = lax.rem(device, two), lax.div(device, two)
        middle = self.chips // 2
        place = chip
        if self.snake:
            place = jnp.where(lax.rem(chip, two) == 0, lax.div(chip, two), self.chips - 1 - lax.div(chip, two))
        sign = 1 - 2 * lax.rem(core + place, two)
        names, values = ["self", "pair"], [device, device + 1 - 2 * core]
        for step in range(-self.rounds, self.rounds + 1):
            owner = lax.rem(place - sign * step + self.chips, jnp.int32(self.chips))
            if self.snake:
                owner = jnp.where(owner < middle, 2 * owner, 2 * (self.chips - 1 - owner) + 1)
            names += [(step, True), (step, False), step]
            half = core if step % 2 == 0 else 1 - core
            values += [2 * owner + half, 2 * owner + 1 - half, lax.div(owner, jnp.int32(key_share))]
        values = lax.optimization_barrier([x.astype(jnp.int32) for x in values])
        self.numbers = dict(zip(names, values))
        return values

    def number(self, name):
        return self.numbers[name].reshape(1)

    def send(self, block, way):
        route = []
        for place in range(self.chips):
            for core in (0, 1):
                ahead = way if (core + place) % 2 == 0 else -way
                to = self.order[(place + ahead) % self.chips]
                route.append((self.order[place] * 2 + core, to * 2 + 1 - core))
        return lax.ppermute(block, "ctx", sorted(route))

    def swap(self, block):
        return lax.ppermute(block, "ctx", [(i, i ^ 1) for i in range(2 * self.chips)])


def after(value, *others):
    return lax.optimization_barrier((value, *others))[0]


def near(x):
    return pltpu.with_memory_space_constraint(x, pltpu.VMEM)


def far(x):
    return pltpu.with_memory_space_constraint(x, pltpu.HBM)


def limit(megabytes):
    return pltpu.CompilerParams(vmem_limit_bytes=megabytes * 1024 * 1024)


def stat_rows(rows):
    return -(-3 * (rows // LANES) // TILE) * TILE


def diagonal():
    shape = (LANES, LANES)
    return lax.broadcasted_iota(jnp.int32, shape, 0) == lax.broadcasted_iota(jnp.int32, shape, 1)


def pack_stats(stats):
    high = [x.astype(BF16).astype(F32) for x in stats]
    rest = [x - h for x, h in zip(stats, high)]
    middle = [x.astype(BF16).astype(F32) for x in rest]
    low = [x - h for x, h in zip(rest, middle)]
    parts = high + middle + low
    parts += [jnp.zeros_like(stats[0])] * (-len(parts) % TILE)
    return jnp.concatenate(parts, axis=0).astype(BF16)


def unpack_stats(ref, rows):
    blocks = rows // LANES
    packed = ref[pl.ds(rows, stat_rows(rows)), :].astype(F32)
    return packed[:blocks] + packed[blocks : 2 * blocks] + packed[2 * blocks : 3 * blocks]


def fetch_columns(group, sources, targets, sems):
    columns = pl.ds(pl.multiple_of(group * LANES, LANES), LANES)
    tokens = sources[0].shape[0]
    copies = []
    for i, source in enumerate(sources):
        target = targets[i // 2].at[pl.ds((i % 2) * tokens, tokens), :]
        copies.append(pltpu.make_async_copy(source.at[:, columns], target, sems.at[i]))
        copies[-1].start()
    return copies


def prepare_kernel(this, pair, last, onehot, bias):
    shape = onehot.shape
    block = lax.broadcasted_iota(jnp.int32, shape, 0) // BLK
    lane = lax.broadcasted_iota(jnp.int32, shape, 1)
    onehot[...] = (block == lane).astype(F32).astype(BF16)
    blocks = shape[0] // BLK // 2
    lane = lax.broadcasted_iota(jnp.int32, bias.shape, 1)
    place = jnp.where(
        lane < blocks, this[0] * blocks + lane, (pair[0] - 1) * blocks + lane
    )
    bias[...] = jnp.where(place <= last[...], 0.0, MASKED).astype(BF16)


def prepare(ring, last, tokens):
    queries = last.shape[0]
    return pl.pallas_call(
        prepare_kernel,
        out_shape=[
            pltpu.VMEM((tokens, LANES), BF16),
            pltpu.VMEM((queries, LANES), BF16),
        ],
        in_specs=[SCALARS, SCALARS, VMEM],
        out_specs=[VMEM] * 2,
        compiler_params=limit(8),
        cost_estimate=took(0.09),
        name="prepare",
    )(ring.number("self"), ring.number("pair"), near(last))


def stage_kernel(source, target, sem):
    copy = pltpu.make_async_copy(source, target, sem)
    copy.start()
    copy.wait()


def stage(weight):
    return pl.pallas_call(
        stage_kernel,
        out_shape=pltpu.VMEM(weight.shape, weight.dtype),
        in_specs=[ANYWHERE],
        out_specs=VMEM,
        scratch_shapes=[pltpu.SemaphoreType.DMA],
        compiler_params=limit(8),
        cost_estimate=took(0.8999999999999999),
        name="stage",
    )(far(weight))


def fetch_kernel(head, k0, k1, v0, v1, key, value, sems):
    for copy in fetch_columns(head[0], (k0, k1, v0, v1), (key, value), sems):
        copy.wait()


def fetch(head, cache):
    shape = pltpu.VMEM((2 * cache[0].shape[0], LANES), BF16)
    return pl.pallas_call(
        fetch_kernel,
        out_shape=[shape, shape],
        in_specs=[SCALARS] + [ANYWHERE] * 4,
        out_specs=[VMEM] * 2,
        scratch_shapes=[pltpu.SemaphoreType.DMA((4,))],
        compiler_params=limit(8),
        cost_estimate=took(0.36),
        name="fetch",
    )(head, far(cache[0]), cache[1], far(cache[2]), cache[3])


def attend_kernel(chunk, parts, q, bias, onehot, key, value, *refs):
    copies = []
    if len(refs) > parts:
        following, *cache = refs[:5]
        outs, (next_key, next_value, sems) = refs[5 : 5 + parts], refs[5 + parts :]
        copies = fetch_columns(following[0], cache, (next_key, next_value), sems)
    else:
        outs = refs
    rows = q.shape[0] // parts
    diag = diagonal()
    biases = jnp.concatenate([bias[...]] * (chunk // bias.shape[0]), axis=0)

    def scores(start):
        query = jnp.concatenate([q[pl.ds(start, chunk), :], biases], axis=1)
        keys = jnp.concatenate([key[...], onehot[...]], axis=1)
        return lax.dot_general(
            query, keys, (((1,), (1,)), ((), ())), preferred_element_type=F32
        )

    starts = range(0, parts * rows, chunk)
    coming, stats = scores(0), []
    for start in starts:
        score = coming
        if start + chunk < parts * rows:
            coming = scores(start + chunk)
        peak = jnp.max(score, axis=1, keepdims=True)
        weights = jnp.exp2(score - peak).astype(BF16)
        values = jnp.concatenate([value[...], jnp.ones(value.shape, BF16)], axis=1)
        sums = jnp.dot(weights, values, preferred_element_type=F32)
        total = sums[:, LANES:]
        out, inside = outs[start // rows], start % rows
        out[pl.ds(inside, chunk), :] = (sums[:, :LANES] / total).astype(BF16)
        level = peak + jnp.log2(total)
        for b in range(chunk // LANES):
            block = level[b * LANES : (b + 1) * LANES]
            stats.append(jnp.sum(jnp.where(diag, block, 0.0), axis=0, keepdims=True))
        if inside + chunk == rows:
            out[pl.ds(rows, stat_rows(rows)), :] = pack_stats(stats)
            stats = []
    for copy in copies:
        copy.wait()


def attend(following, q, parts, bias, onehot, head, cache):
    rows, width = q.shape[0] // parts, q.shape[1]
    chunk = math.gcd(rows, 256)
    shapes = [pltpu.VMEM((rows + stat_rows(rows), width), BF16)] * parts
    arrays = [near(x) for x in (q, bias, onehot, *head)]
    specs, scratch = [VMEM] * 5, []
    if following is not None:
        shapes += [pltpu.VMEM(head[0].shape, BF16)] * 2
        arrays += [following, far(cache[0]), cache[1], far(cache[2]), cache[3]]
        specs += [SCALARS] + [ANYWHERE] * 4
        scratch = [pltpu.SemaphoreType.DMA((4,))]
    out = pl.pallas_call(
        functools.partial(attend_kernel, chunk, parts),
        out_shape=shapes,
        in_specs=specs,
        out_specs=[VMEM] * len(shapes),
        scratch_shapes=scratch,
        compiler_params=limit(16),
        cost_estimate=pl.CostEstimate(
            flops=16 * parts * rows * head[0].shape[0] * width,
            bytes_accessed=8 * head[0].size,
            transcendentals=parts * rows * head[0].shape[0],
        ),
        name="attend",
    )(*arrays)
    return out[:parts], out[parts:]


def spread(diag, row):
    high = row.astype(BF16).astype(F32)
    ones = jnp.ones((LANES, LANES), BF16)
    return sum(
        jnp.dot(jnp.where(diag, x, 0.0).astype(BF16), ones, preferred_element_type=F32)
        for x in (high, row - high)
    )


def merged(diag, block, one, one_stat, two, two_stat):
    peak = jnp.maximum(one_stat, two_stat)
    one_part, two_part = jnp.exp2(one_stat - peak), jnp.exp2(two_stat - peak)
    total = one_part + two_part
    share = spread(diag, one_part / total)
    here = pl.ds(block * LANES, LANES)
    one, two = one[here, :].astype(F32), two[here, :].astype(F32)
    return two + share * (one - two), peak + jnp.log2(total)


def merge_kernel(rows, one, two, out):
    diag = diagonal()
    one_stats, two_stats = unpack_stats(one, rows), unpack_stats(two, rows)
    stats = []
    for b in range(rows // LANES):
        value, stat = merged(diag, b, one, one_stats[b : b + 1], two, two_stats[b : b + 1])
        out[pl.ds(b * LANES, LANES), :] = value.astype(BF16)
        stats.append(stat)
    out[pl.ds(rows, stat_rows(rows)), :] = pack_stats(stats)


def merge(rows, one, two):
    return pl.pallas_call(
        functools.partial(merge_kernel, rows),
        out_shape=pltpu.VMEM(two.shape, BF16),
        in_specs=[VMEM, VMEM],
        out_specs=VMEM,
        cost_estimate=took(0.075),
        compiler_params=limit(8),
        name="merge",
    )(near(one), near(two))


def finish_kernel(rows, queries, *refs):
    parts, out = refs[:-1], refs[-1]
    diag = diagonal()
    width = parts[0].shape[1]
    stats = [unpack_stats(part, rows) for part in parts]
    for b in range(rows // LANES):
        here = pl.ds(b * LANES, LANES)
        levels = [stat[b : b + 1] for stat in stats]
        peak = functools.reduce(jnp.maximum, levels)
        shares = [jnp.exp2(level - peak) for level in levels]
        total = sum(shares)
        value = sum(
            spread(diag, share / total) * part[here, :].astype(F32)
            for share, part in zip(shares, parts)
        ).astype(BF16)
        for piece in range(LANES // queries):
            head = (b * LANES) // queries + piece
            out[:, pl.ds(head * width, width)] = value[piece * queries : (piece + 1) * queries]


def finish(rows, queries, parts):
    width = parts[0].shape[1]
    return pl.pallas_call(
        functools.partial(finish_kernel, rows, queries),
        out_shape=pltpu.VMEM((queries, rows // queries * width), BF16),
        in_specs=[VMEM] * len(parts),
        out_specs=VMEM,
        compiler_params=limit(8),
        cost_estimate=took(0.105),
        name="finish",
    )(*[near(x) for x in parts])


def weight_rows(weight, block, target, sem):
    width = target.shape[0]
    start = pl.multiple_of(block[0] * width, width)
    copy = pltpu.make_async_copy(weight.at[pl.ds(start, width), :], target, sem)
    copy.start()
    return copy


def project_kernel(plan, *refs):
    queries, features, scale, carried, begun, count, coming, fetched = plan
    refs = list(refs)
    take = lambda n: [refs.pop(0) for _ in range(n)]
    blocks, later = take(0 if fetched else count), take(coming)
    parts = take(count)
    gains, row = (parts, queries) if carried else (take(count), queries + 1)
    weights = take(count) if fetched else take(1)
    state = take(2 if begun else 0)
    head_gain = take(1 if scale else 0)
    outs, targets = take(1 if features else 2), take(coming)
    copies = []
    if not fetched:
        pieces, sems = take(2)
        copies = [
            weight_rows(weights[0], block, pieces.at[i], sems.at[i])
            for i, block in enumerate(blocks)
        ]
        weights_at = [pieces.at[i] for i in range(count)]
        ahead = [
            weight_rows(weights[0], block, target, sems.at[count + i])
            for i, (block, target) in enumerate(zip(later, targets))
        ]
    else:
        weights_at, ahead = weights, []
    total, square = (state[0][...], state[1][...]) if begun else (0.0, 0.0)
    scaled = []
    for part, gain in zip(parts, gains):
        values = part[...][:queries].astype(F32)
        scaled.append((values * gain[...][row : row + 1].astype(F32)).astype(BF16))
        for lane in range(0, part.shape[1], LANES):
            square += values[:, lane : lane + LANES] * values[:, lane : lane + LANES]
    for i, weight in enumerate(weights_at):
        if copies:
            copies[i].wait()
        total += jnp.dot(scaled[i], weight[...], preferred_element_type=F32)
    if not features:
        outs[0][...] = total
        outs[1][...] = square
    else:
        factor = lax.rsqrt(jnp.sum(square, axis=1, keepdims=True) / features + EPSILON)
        if not scale:
            outs[0][...] = (total * factor).astype(BF16)
        else:
            gain = head_gain[0][...].astype(F32) * scale
            width = gain.shape[1]
            for head in range(total.shape[1] // width):
                value = total[:, head * width : (head + 1) * width] * factor
                mean = jnp.mean(value * value, axis=1, keepdims=True)
                outs[0][pl.ds(head * queries, queries), :] = (
                    value * lax.rsqrt(mean + EPSILON) * gain
                ).astype(BF16)
    for copy in ahead:
        copy.wait()


def project(queries, blocks, later, parts, gains, weight, state, fetched=None, last=False, head_gain=None):
    count, depth, width = len(parts), parts[0].shape[1], weight.shape[1]
    scale = 0.0
    shapes = [pltpu.VMEM((queries, width), F32), pltpu.VMEM((queries, LANES), F32)]
    scalars = [] if fetched else [*blocks, *later]
    arrays = [near(x) for x in (*parts, *(gains or ()), *(fetched or ()))]
    specs = [VMEM] * len(arrays)
    if not fetched:
        arrays.append(far(weight))
        specs.append(ANYWHERE)
    arrays += [near(x) for x in state or ()]
    if head_gain is not None:
        arrays.append(near(head_gain[None, :]))
        size = head_gain.shape[0]
        scale = size**-0.5 * math.log2(math.e)
        shapes = [pltpu.VMEM((width // size * queries, size), BF16)]
    elif last:
        shapes = [jax.ShapeDtypeStruct((queries, width), BF16)]
    specs += [VMEM] * (len(arrays) - len(specs))
    shapes += [pltpu.VMEM((depth, width), BF16)] * len(later)
    features = weight.shape[0] if last else 0
    plan = queries, features, scale, not gains, bool(state), count, len(later), bool(fetched)
    scratch = []
    if not fetched:
        scratch = [
            pltpu.VMEM((count, depth, width), BF16),
            pltpu.SemaphoreType.DMA((count + len(later),)),
        ]
    out = pl.pallas_call(
        functools.partial(project_kernel, plan),
        out_shape=shapes,
        in_specs=[SCALARS] * len(scalars) + specs,
        out_specs=[VMEM] * len(shapes),
        scratch_shapes=scratch,
        compiler_params=limit(16),
        cost_estimate=took(0.6),
        name="project",
    )(*scalars, *arrays)
    edge = len(out) - len(later)
    return out[:edge], out[edge:]


def gather_project(ring, queries, own, other, carriers, weight, beside=None, head_gain=None, meanwhile=None):
    arrived, waiting, state = {}, [], None
    rounds = ring.rounds
    final = [(rounds, True), (-rounds, False), (rounds - 1, False), (1 - rounds, True)]

    def flush(names, later=(), **how):
        waiting[:] = [name for name in waiting if name not in names]
        return project(
            queries,
            [ring.number(name) for name in names],
            [ring.number(name) for name in later],
            [arrived[name] for name in names],
            carriers and [carriers[name] for name in names],
            weight,
            state,
            **how,
        )

    def keep(name, part):
        arrived[name] = part
        waiting.append(name)

    keep((0, True), own)
    keep((0, False), other)
    for step in range(1, rounds + 1):
        own = ring.send(after(own, *(beside or {}).get(step, ()), *(state or ())), 1)
        if step < rounds:
            other = ring.send(other, 1)
            if len(waiting) > 16:
                state, _ = flush([name for name in waiting if abs(name[0]) < step - 1])
            keep((step, True), own)
            keep((-step, False), ring.swap(own))
            keep((step, False), other)
            if step < rounds - 1:
                keep((-step, True), ring.swap(other))
    state, fetched = flush([name for name in waiting if name not in final], final)
    before = arrived[rounds - 1, True]
    own, other, before = after(own, *state), after(other, own, *state), after(before, own, *state)
    extra = meanwhile(own) if meanwhile else ()
    keep((rounds, True), own)
    keep((-rounds, False), after(ring.swap(own), *extra))
    keep((1 - rounds, True), ring.swap(other))
    (result,), _ = flush(final, fetched=fetched, last=True, head_gain=head_gain)
    return result, arrived, extra


def mix_kernel(count, *refs):
    blocks, (one, two, one_weight, two_weight) = refs[:count], refs[count : count + 4]
    for block, out in zip(blocks, refs[count + 4 :]):
        width = out.shape[1]
        columns = pl.ds(pl.multiple_of(block[0] * width, width), width)
        value = jnp.dot(one[...], one_weight[:, columns], preferred_element_type=F32)
        value += jnp.dot(two[...], two_weight[:, columns], preferred_element_type=F32)
        out[...] = value.astype(out.dtype)


def mix(blocks, width, kind, one, two, one_weight, two_weight):
    return pl.pallas_call(
        functools.partial(mix_kernel, len(blocks)),
        out_shape=[pltpu.VMEM((one.shape[0], width), kind)] * len(blocks),
        in_specs=[SCALARS] * len(blocks) + [VMEM] * 4,
        out_specs=[VMEM] * len(blocks),
        compiler_params=limit(8),
        cost_estimate=took(0.18),
        name="mix",
    )(*blocks, *[near(x) for x in (one, two, one_weight, two_weight)])


def add_kernel(*refs):
    rows = refs[-1].shape[0]
    refs[-1][...] = sum(ref[...][:rows].astype(F32) for ref in refs[:-1]).astype(BF16)


def add(*parts):
    return pl.pallas_call(
        add_kernel,
        out_shape=pltpu.VMEM(parts[0].shape, BF16),
        in_specs=[VMEM] * len(parts),
        out_specs=VMEM,
        compiler_params=limit(8),
        cost_estimate=took(0.03),
        name="add",
    )(*[near(x) for x in parts])


def join_kernel(one, two, out):
    rows = one.shape[0]
    out[:rows] = one[...]
    out[rows:] = two[...]


def join(one, two):
    return pl.pallas_call(
        join_kernel,
        out_shape=pltpu.VMEM((2 * one.shape[0], one.shape[1]), one.dtype),
        in_specs=[VMEM, VMEM],
        out_specs=VMEM,
        compiler_params=limit(8),
        cost_estimate=took(0.03),
        name="join",
    )(near(one), near(two))


def first_half_kernel(both, out):
    out[...] = both[: out.shape[0]]


def first_half(both):
    return pl.pallas_call(
        first_half_kernel,
        out_shape=pltpu.VMEM((both.shape[0] // 2, both.shape[1]), both.dtype),
        in_specs=[VMEM],
        out_specs=VMEM,
        compiler_params=limit(8),
        cost_estimate=took(0.03),
        name="first_half",
    )(near(both))


def on_device(
    columns,
    hidden,
    attn_gain,
    q_weight,
    q_gain,
    key_cache,
    value_cache,
    block_limit,
    out_weight,
    next_gain,
    next_weight,
):
    ring = Ring(lax.axis_size("ctx"), columns)
    rounds = ring.rounds
    queries, here = hidden.shape
    head_dim = q_gain.shape[0]
    heads_here = q_weight.shape[1] // head_dim
    rows = heads_here * queries
    kv_heads = key_cache.shape[1] // head_dim
    group_size = heads_here * 2 * ring.chips // kv_heads

    numbers = ring.locate(group_size // (2 * heads_here))

    row = jnp.arange(queries + 2, dtype=jnp.int32)[:, None]
    own = jnp.where(
        row < queries,
        jnp.pad(hidden, ((0, 2), (0, 0))),
        jnp.where(row == queries, attn_gain[None, :], next_gain[None, :]),
    )
    last = jnp.broadcast_to(block_limit[:, None], (queries, LANES))
    own, last = after(own, *numbers), after(last, *numbers)
    other = ring.swap(own)
    other_keys = ring.swap(after(key_cache, other))
    other_values = ring.swap(after(value_cache, other))
    cache = (key_cache, other_keys, value_cache, other_values)
    beside = {rounds - 1: (other_keys,), rounds: (other_values,)}

    def meanwhile(token):
        onehot, bias = prepare(ring, after(last, token), 2 * key_cache.shape[0])
        ready = after(key_cache, token), other_keys, after(value_cache, token), other_values
        return onehot, bias, *fetch(ring.number(0), ready)

    own_heads, carriers, (onehot, bias, *head) = gather_project(
        ring, queries, own, other, None, q_weight, beside, q_gain, meanwhile
    )
    other_weight = ring.swap(after(out_weight, own_heads))

    travelling, running, done = own_heads, None, own_heads
    for step in range(ring.chips):
        last = step + 1 == ring.chips
        if not last:
            coming = ring.send(travelling, 1)
        following = step + 1 if step < rounds else step + 1 - ring.chips
        (part,), head = attend(
            None if last else ring.number(following),
            after(travelling, done),
            1,
            bias,
            onehot,
            head,
            cache,
        )
        if step == 0:
            local = part
        else:
            running = ring.send(part if running is None else merge(rows, running, part), 1)
        travelling, done = coming, part
    attended = finish(rows, queries, (running, local))
    attended_other = ring.swap(attended)

    def mixed(kind, places):
        blocks = [ring.number(place) for place in places]
        weights = (out_weight, other_weight)
        parts = mix(blocks, here, kind, attended, attended_other, *weights)
        return dict(zip(places, parts))

    first = [(rounds, True), (rounds - 1, False)]
    places = [(step, mine) for step in range(rounds - 1, -1, -1) for mine in (True, False)]
    shares = mixed(BF16, first) | mixed(F32, [place for place in places if place not in first])
    own, other = (ring.send(shares[place], -1) for place in first)
    for step in range(rounds - 1, 0, -1):
        own = ring.send(add(shares[step, True], own), -1)
        if step > 1:
            other = ring.send(add(shares[step - 1, False], other), -1)
    own_far, other_far = ring.swap(own), ring.swap(other)
    new_own = add(shares[0, True], own, other_far, carriers[0, True])
    new_other = add(shares[0, False], other, own_far, carriers[0, False])
    next_queries, _, _ = gather_project(ring, queries, new_own, new_other, carriers, next_weight)
    return new_own, next_queries


def solution(mesh):
    in_specs = (
        P("groups", "ctx"),
        P("ctx"),
        P(None, "ctx"),
        P(),
        P(("groups", "ctx"), None),
        P(("groups", "ctx"), None),
        P("groups"),
        P("ctx", None),
        P("ctx"),
        P(None, "ctx"),
    )
    out_specs = (P("groups", "ctx"), P("groups", "ctx"))
    columns = 2 if mesh.shape["groups"] == 2 else 1
    return jax.shard_map(
        functools.partial(on_device, columns),
        mesh=mesh,
        in_specs=in_specs,
        out_specs=out_specs,
        check_vma=False,
    )
```

```python
import functools
import math

import jax
import jax.numpy as jnp
from jax import lax
from jax.experimental import pallas as pl
from jax.experimental.pallas import tpu as pltpu
from jax.sharding import PartitionSpec as P

BLK = 128
EPSILON = 1e-05
MASKED = -1e30
LANES = 128
TILE = 16
BF16 = jnp.bfloat16
F32 = jnp.float32
VMEM = pl.BlockSpec(memory_space=pltpu.VMEM)
ANYWHERE = pl.BlockSpec(memory_space=pl.ANY)
SCALARS = pl.BlockSpec(memory_space=pltpu.SMEM)


FREE = pl.CostEstimate(flops=0, bytes_accessed=0, transcendentals=0)


def took(microseconds):
    return pl.CostEstimate(
        flops=int(microseconds * 1.15e9), bytes_accessed=0, transcendentals=0
    )


class Ring:
    def __init__(self, devices, columns):
        self.chips = devices // 2
        self.rounds = self.chips // 2
        self.snake = columns == 2 and self.chips % 2 == 0
        if self.snake:
            self.order = list(range(0, self.chips, 2)) + list(range(1, self.chips, 2))[::-1]
        else:
            self.order = list(range(self.chips))

    def locate(self, key_share):
        device = lax.axis_index("ctx")
        two = jnp.int32(2)
        core, chip = lax.rem(device, two), lax.div(device, two)
        middle = self.chips // 2
        place = chip
        if self.snake:
            place = jnp.where(lax.rem(chip, two) == 0, lax.div(chip, two), self.chips - 1 - lax.div(chip, two))
        sign = 1 - 2 * lax.rem(core + place, two)
        names, values = ["self", "pair"], [device, device + 1 - 2 * core]
        for step in range(-self.rounds, self.rounds + 1):
            owner = lax.rem(place - sign * step + self.chips, jnp.int32(self.chips))
            if self.snake:
                owner = jnp.where(owner < middle, 2 * owner, 2 * (self.chips - 1 - owner) + 1)
            names += [(step, True), (step, False), step]
            half = core if step % 2 == 0 else 1 - core
            values += [2 * owner + half, 2 * owner + 1 - half, lax.div(owner, jnp.int32(key_share))]
        values = lax.optimization_barrier([x.astype(jnp.int32) for x in values])
        self.numbers = dict(zip(names, values))
        return values

    def number(self, name):
        return self.numbers[name].reshape(1)

    def send(self, block, way):
        route = []
        for place in range(self.chips):
            for core in (0, 1):
                ahead = way if (core + place) % 2 == 0 else -way
                to = self.order[(place + ahead) % self.chips]
                route.append((self.order[place] * 2 + core, to * 2 + 1 - core))
        return lax.ppermute(block, "ctx", sorted(route))

    def swap(self, block):
        return lax.ppermute(block, "ctx", [(i, i ^ 1) for i in range(2 * self.chips)])


def after(value, *others):
    return lax.optimization_barrier((value, *others))[0]


def near(x):
    return pltpu.with_memory_space_constraint(x, pltpu.VMEM)


def far(x):
    return pltpu.with_memory_space_constraint(x, pltpu.HBM)


def limit(megabytes):
    return pltpu.CompilerParams(vmem_limit_bytes=megabytes * 1024 * 1024)


def stat_rows(rows):
    return -(-3 * (rows // LANES) // TILE) * TILE


def diagonal():
    shape = (LANES, LANES)
    return lax.broadcasted_iota(jnp.int32, shape, 0) == lax.broadcasted_iota(jnp.int32, shape, 1)


def pack_stats(stats):
    high = [x.astype(BF16).astype(F32) for x in stats]
    rest = [x - h for x, h in zip(stats, high)]
    middle = [x.astype(BF16).astype(F32) for x in rest]
    low = [x - h for x, h in zip(rest, middle)]
    parts = high + middle + low
    parts += [jnp.zeros_like(stats[0])] * (-len(parts) % TILE)
    return jnp.concatenate(parts, axis=0).astype(BF16)


def unpack_stats(ref, rows):
    blocks = rows // LANES
    packed = ref[pl.ds(rows, stat_rows(rows)), :].astype(F32)
    return packed[:blocks] + packed[blocks : 2 * blocks] + packed[2 * blocks : 3 * blocks]


def fetch_columns(group, sources, targets, sems):
    columns = pl.ds(pl.multiple_of(group * LANES, LANES), LANES)
    tokens = sources[0].shape[0]
    copies = []
    for i, source in enumerate(sources):
        target = targets[i // 2].at[pl.ds((i % 2) * tokens, tokens), :]
        copies.append(pltpu.make_async_copy(source.at[:, columns], target, sems.at[i]))
        copies[-1].start()
    return copies


def prepare_kernel(this, pair, last, onehot, bias):
    shape = onehot.shape
    block = lax.broadcasted_iota(jnp.int32, shape, 0) // BLK
    lane = lax.broadcasted_iota(jnp.int32, shape, 1)
    onehot[...] = (block == lane).astype(F32).astype(BF16)
    blocks = shape[0] // BLK // 2
    lane = lax.broadcasted_iota(jnp.int32, bias.shape, 1)
    place = jnp.where(
        lane < blocks, this[0] * blocks + lane, (pair[0] - 1) * blocks + lane
    )
    bias[...] = jnp.where(place <= last[...], 0.0, MASKED).astype(BF16)


def prepare(ring, last, tokens):
    queries = last.shape[0]
    return pl.pallas_call(
        prepare_kernel,
        out_shape=[
            pltpu.VMEM((tokens, LANES), BF16),
            pltpu.VMEM((queries, LANES), BF16),
        ],
        in_specs=[SCALARS, SCALARS, VMEM],
        out_specs=[VMEM] * 2,
        compiler_params=limit(8),
        cost_estimate=took(0.09),
        name="prepare",
    )(ring.number("self"), ring.number("pair"), near(last))


def stage_kernel(source, target, sem):
    copy = pltpu.make_async_copy(source, target, sem)
    copy.start()
    copy.wait()


def stage(weight):
    return pl.pallas_call(
        stage_kernel,
        out_shape=pltpu.VMEM(weight.shape, weight.dtype),
        in_specs=[ANYWHERE],
        out_specs=VMEM,
        scratch_shapes=[pltpu.SemaphoreType.DMA],
        compiler_params=limit(8),
        cost_estimate=took(0.8999999999999999),
        name="stage",
    )(far(weight))


def fetch_kernel(head, k0, k1, v0, v1, key, value, sems):
    for copy in fetch_columns(head[0], (k0, k1, v0, v1), (key, value), sems):
        copy.wait()


def fetch(head, cache):
    shape = pltpu.VMEM((2 * cache[0].shape[0], LANES), BF16)
    return pl.pallas_call(
        fetch_kernel,
        out_shape=[shape, shape],
        in_specs=[SCALARS] + [ANYWHERE] * 4,
        out_specs=[VMEM] * 2,
        scratch_shapes=[pltpu.SemaphoreType.DMA((4,))],
        compiler_params=limit(8),
        cost_estimate=took(0.36),
        name="fetch",
    )(head, far(cache[0]), cache[1], far(cache[2]), cache[3])


def attend_kernel(chunk, parts, q, bias, onehot, key, value, *refs):
    copies = []
    if len(refs) > parts:
        following, *cache = refs[:5]
        outs, (next_key, next_value, sems) = refs[5 : 5 + parts], refs[5 + parts :]
        copies = fetch_columns(following[0], cache, (next_key, next_value), sems)
    else:
        outs = refs
    rows = q.shape[0] // parts
    diag = diagonal()
    biases = jnp.concatenate([bias[...]] * (chunk // bias.shape[0]), axis=0)

    def scores(start):
        query = jnp.concatenate([q[pl.ds(start, chunk), :], biases], axis=1)
        keys = jnp.concatenate([key[...], onehot[...]], axis=1)
        return lax.dot_general(
            query, keys, (((1,), (1,)), ((), ())), preferred_element_type=F32
        )

    starts = range(0, parts * rows, chunk)
    coming, stats = scores(0), []
    for start in starts:
        score = coming
        if start + chunk < parts * rows:
            coming = scores(start + chunk)
        peak = jnp.max(score, axis=1, keepdims=True)
        weights = jnp.exp2(score - peak).astype(BF16)
        values = jnp.concatenate([value[...], jnp.ones(value.shape, BF16)], axis=1)
        sums = jnp.dot(weights, values, preferred_element_type=F32)
        total = sums[:, LANES:]
        out, inside = outs[start // rows], start % rows
        out[pl.ds(inside, chunk), :] = (sums[:, :LANES] / total).astype(BF16)
        level = peak + jnp.log2(total)
        for b in range(chunk // LANES):
            block = level[b * LANES : (b + 1) * LANES]
            stats.append(jnp.sum(jnp.where(diag, block, 0.0), axis=0, keepdims=True))
        if inside + chunk == rows:
            out[pl.ds(rows, stat_rows(rows)), :] = pack_stats(stats)
            stats = []
    for copy in copies:
        copy.wait()


def attend(following, q, parts, bias, onehot, head, cache):
    rows, width = q.shape[0] // parts, q.shape[1]
    chunk = math.gcd(rows, 256)
    shapes = [pltpu.VMEM((rows + stat_rows(rows), width), BF16)] * parts
    arrays = [near(x) for x in (q, bias, onehot, *head)]
    specs, scratch = [VMEM] * 5, []
    if following is not None:
        shapes += [pltpu.VMEM(head[0].shape, BF16)] * 2
        arrays += [following, far(cache[0]), cache[1], far(cache[2]), cache[3]]
        specs += [SCALARS] + [ANYWHERE] * 4
        scratch = [pltpu.SemaphoreType.DMA((4,))]
    out = pl.pallas_call(
        functools.partial(attend_kernel, chunk, parts),
        out_shape=shapes,
        in_specs=specs,
        out_specs=[VMEM] * len(shapes),
        scratch_shapes=scratch,
        compiler_params=limit(16),
        cost_estimate=pl.CostEstimate(
            flops=32 * parts * rows * head[0].shape[0] * width,
            bytes_accessed=8 * head[0].size,
            transcendentals=parts * rows * head[0].shape[0],
        ),
        name="attend",
    )(*arrays)
    return out[:parts], out[parts:]


def spread(diag, row):
    high = row.astype(BF16).astype(F32)
    ones = jnp.ones((LANES, LANES), BF16)
    return sum(
        jnp.dot(jnp.where(diag, x, 0.0).astype(BF16), ones, preferred_element_type=F32)
        for x in (high, row - high)
    )


def merged(diag, block, one, one_stat, two, two_stat):
    peak = jnp.maximum(one_stat, two_stat)
    one_part, two_part = jnp.exp2(one_stat - peak), jnp.exp2(two_stat - peak)
    total = one_part + two_part
    share = spread(diag, one_part / total)
    here = pl.ds(block * LANES, LANES)
    one, two = one[here, :].astype(F32), two[here, :].astype(F32)
    return two + share * (one - two), peak + jnp.log2(total)


def merge_kernel(rows, one, two, out):
    diag = diagonal()
    one_stats, two_stats = unpack_stats(one, rows), unpack_stats(two, rows)
    stats = []
    for b in range(rows // LANES):
        value, stat = merged(diag, b, one, one_stats[b : b + 1], two, two_stats[b : b + 1])
        out[pl.ds(b * LANES, LANES), :] = value.astype(BF16)
        stats.append(stat)
    out[pl.ds(rows, stat_rows(rows)), :] = pack_stats(stats)


def merge(rows, one, two):
    return pl.pallas_call(
        functools.partial(merge_kernel, rows),
        out_shape=pltpu.VMEM(two.shape, BF16),
        in_specs=[VMEM, VMEM],
        out_specs=VMEM,
        cost_estimate=took(0.075),
        compiler_params=limit(8),
        name="merge",
    )(near(one), near(two))


def finish_kernel(rows, queries, *refs):
    parts, out = refs[:-1], refs[-1]
    diag = diagonal()
    width = parts[0].shape[1]
    stats = [unpack_stats(part, rows) for part in parts]
    for b in range(rows // LANES):
        here = pl.ds(b * LANES, LANES)
        levels = [stat[b : b + 1] for stat in stats]
        peak = functools.reduce(jnp.maximum, levels)
        shares = [jnp.exp2(level - peak) for level in levels]
        total = sum(shares)
        value = sum(
            spread(diag, share / total) * part[here, :].astype(F32)
            for share, part in zip(shares, parts)
        ).astype(BF16)
        for piece in range(LANES // queries):
            head = (b * LANES) // queries + piece
            out[:, pl.ds(head * width, width)] = value[piece * queries : (piece + 1) * queries]


def finish(rows, queries, parts):
    width = parts[0].shape[1]
    return pl.pallas_call(
        functools.partial(finish_kernel, rows, queries),
        out_shape=pltpu.VMEM((queries, rows // queries * width), BF16),
        in_specs=[VMEM] * len(parts),
        out_specs=VMEM,
        compiler_params=limit(8),
        cost_estimate=took(0.105),
        name="finish",
    )(*[near(x) for x in parts])


def weight_rows(weight, block, target, sem):
    width = target.shape[0]
    start = pl.multiple_of(block[0] * width, width)
    copy = pltpu.make_async_copy(weight.at[pl.ds(start, width), :], target, sem)
    copy.start()
    return copy


def project_kernel(plan, *refs):
    queries, features, scale, carried, begun, count, coming, fetched, resident = plan
    refs = list(refs)
    take = lambda n: [refs.pop(0) for _ in range(n)]
    blocks, later = take(0 if fetched else count), take(coming)
    parts = take(count)
    gains, row = (parts, queries) if carried else (take(count), queries + 1)
    weights = take(count) if fetched else take(1)
    state = take(2 if begun else 0)
    head_gain = take(1 if scale else 0)
    outs, targets = take(1 if features else 2), take(coming)
    copies = []
    if resident:
        depth = parts[0].shape[1]
        starts = [pl.multiple_of(block[0] * depth, depth) for block in blocks]
        weights_at, ahead = [weights[0].at[pl.ds(start, depth), :] for start in starts], []
    elif not fetched:
        pieces, sems = take(2)
        copies = [
            weight_rows(weights[0], block, pieces.at[i], sems.at[i])
            for i, block in enumerate(blocks)
        ]
        weights_at = [pieces.at[i] for i in range(count)]
        ahead = [
            weight_rows(weights[0], block, target, sems.at[count + i])
            for i, (block, target) in enumerate(zip(later, targets))
        ]
    else:
        weights_at, ahead = weights, []
    total, square = (state[0][...], state[1][...]) if begun else (0.0, 0.0)
    scaled = []
    for part, gain in zip(parts, gains):
        values = part[...][:queries].astype(F32)
        scaled.append((values * gain[...][row : row + 1].astype(F32)).astype(BF16))
        for lane in range(0, part.shape[1], LANES):
            square += values[:, lane : lane + LANES] * values[:, lane : lane + LANES]
    for i, weight in enumerate(weights_at):
        if copies:
            copies[i].wait()
        total += jnp.dot(scaled[i], weight[...], preferred_element_type=F32)
    if not features:
        outs[0][...] = total
        outs[1][...] = square
    else:
        factor = lax.rsqrt(jnp.sum(square, axis=1, keepdims=True) / features + EPSILON)
        if not scale:
            outs[0][...] = (total * factor).astype(BF16)
        else:
            gain = head_gain[0][...].astype(F32) * scale
            width = gain.shape[1]
            for head in range(total.shape[1] // width):
                value = total[:, head * width : (head + 1) * width] * factor
                mean = jnp.mean(value * value, axis=1, keepdims=True)
                outs[0][pl.ds(head * queries, queries), :] = (
                    value * lax.rsqrt(mean + EPSILON) * gain
                ).astype(BF16)
    for copy in ahead:
        copy.wait()


def project(queries, blocks, later, parts, gains, weight, state, fetched=None, last=False, head_gain=None, resident=False):
    count, depth, width = len(parts), parts[0].shape[1], weight.shape[1]
    scale = 0.0
    shapes = [pltpu.VMEM((queries, width), F32), pltpu.VMEM((queries, LANES), F32)]
    scalars = [] if fetched else [*blocks, *later]
    arrays = [near(x) for x in (*parts, *(gains or ()), *(fetched or ()))]
    specs = [VMEM] * len(arrays)
    if not fetched:
        arrays.append(near(weight) if resident else far(weight))
        specs.append(VMEM if resident else ANYWHERE)
    arrays += [near(x) for x in state or ()]
    if head_gain is not None:
        arrays.append(near(head_gain[None, :]))
        size = head_gain.shape[0]
        scale = size**-0.5 * math.log2(math.e)
        shapes = [pltpu.VMEM((width // size * queries, size), BF16)]
    elif last:
        shapes = [jax.ShapeDtypeStruct((queries, width), BF16)]
    specs += [VMEM] * (len(arrays) - len(specs))
    shapes += [pltpu.VMEM((depth, width), BF16)] * len(later)
    features = weight.shape[0] if last else 0
    plan = queries, features, scale, not gains, bool(state), count, len(later), bool(fetched), resident
    scratch = []
    if not fetched and not resident:
        scratch = [
            pltpu.VMEM((count, depth, width), BF16),
            pltpu.SemaphoreType.DMA((count + len(later),)),
        ]
    out = pl.pallas_call(
        functools.partial(project_kernel, plan),
        out_shape=shapes,
        in_specs=[SCALARS] * len(scalars) + specs,
        out_specs=[VMEM] * len(shapes),
        scratch_shapes=scratch,
        compiler_params=limit(16),
        cost_estimate=took(0.6),
        name="project",
    )(*scalars, *arrays)
    edge = len(out) - len(later)
    return out[:edge], out[edge:]


def gather_project(ring, queries, own, other, carriers, weight, beside=None, head_gain=None, meanwhile=None):
    arrived, waiting, state = {}, [], None
    rounds = ring.rounds
    final = [(rounds, True), (-rounds, False), (rounds - 1, False), (1 - rounds, True)]

    def flush(names, later=(), **how):
        waiting[:] = [name for name in waiting if name not in names]
        return project(
            queries,
            [ring.number(name) for name in names],
            [ring.number(name) for name in later],
            [arrived[name] for name in names],
            carriers and [carriers[name] for name in names],
            weight,
            state,
            resident=bool(carriers),
            **how,
        )

    def keep(name, part):
        arrived[name] = part
        waiting.append(name)

    keep((0, True), own)
    keep((0, False), other)
    for step in range(1, rounds + 1):
        own = ring.send(after(own, *(beside or {}).get(step, ()), *(state or ())), 1)
        if step < rounds:
            other = ring.send(other, 1)
            if len(waiting) > 16:
                state, _ = flush([name for name in waiting if abs(name[0]) < step - 1])
            keep((step, True), own)
            keep((-step, False), ring.swap(own))
            keep((step, False), other)
            if step < rounds - 1:
                keep((-step, True), ring.swap(other))
    state, fetched = flush([name for name in waiting if name not in final], () if carriers else final)
    before = arrived[rounds - 1, True]
    own, other, before = after(own, *state), after(other, own, *state), after(before, own, *state)
    extra = meanwhile(own) if meanwhile else ()
    keep((rounds, True), own)
    keep((-rounds, False), after(ring.swap(own), *extra))
    keep((1 - rounds, True), ring.swap(other))
    (result,), _ = flush(final, fetched=fetched, last=True, head_gain=head_gain)
    return result, arrived, extra


def mix_kernel(count, *refs):
    blocks, (one, two, one_weight, two_weight) = refs[:count], refs[count : count + 4]
    for block, out in zip(blocks, refs[count + 4 :]):
        width = out.shape[1]
        columns = pl.ds(pl.multiple_of(block[0] * width, width), width)
        value = jnp.dot(one[...], one_weight[:, columns], preferred_element_type=F32)
        value += jnp.dot(two[...], two_weight[:, columns], preferred_element_type=F32)
        out[...] = value.astype(out.dtype)


def mix(blocks, width, kind, one, two, one_weight, two_weight):
    return pl.pallas_call(
        functools.partial(mix_kernel, len(blocks)),
        out_shape=[pltpu.VMEM((one.shape[0], width), kind)] * len(blocks),
        in_specs=[SCALARS] * len(blocks) + [VMEM] * 4,
        out_specs=[VMEM] * len(blocks),
        compiler_params=limit(8),
        cost_estimate=took(0.18),
        name="mix",
    )(*blocks, *[near(x) for x in (one, two, one_weight, two_weight)])


def add_kernel(*refs):
    rows = refs[-1].shape[0]
    refs[-1][...] = sum(ref[...][:rows].astype(F32) for ref in refs[:-1]).astype(BF16)


def add(*parts):
    return pl.pallas_call(
        add_kernel,
        out_shape=pltpu.VMEM(parts[0].shape, BF16),
        in_specs=[VMEM] * len(parts),
        out_specs=VMEM,
        compiler_params=limit(8),
        cost_estimate=took(0.03),
        name="add",
    )(*[near(x) for x in parts])


def join_kernel(one, two, out):
    rows = one.shape[0]
    out[:rows] = one[...]
    out[rows:] = two[...]


def join(one, two):
    return pl.pallas_call(
        join_kernel,
        out_shape=pltpu.VMEM((2 * one.shape[0], one.shape[1]), one.dtype),
        in_specs=[VMEM, VMEM],
        out_specs=VMEM,
        compiler_params=limit(8),
        cost_estimate=took(0.03),
        name="join",
    )(near(one), near(two))


def first_half_kernel(both, out):
    out[...] = both[: out.shape[0]]


def first_half(both):
    return pl.pallas_call(
        first_half_kernel,
        out_shape=pltpu.VMEM((both.shape[0] // 2, both.shape[1]), both.dtype),
        in_specs=[VMEM],
        out_specs=VMEM,
        compiler_params=limit(8),
        cost_estimate=took(0.03),
        name="first_half",
    )(near(both))


def on_device(
    columns,
    hidden,
    attn_gain,
    q_weight,
    q_gain,
    key_cache,
    value_cache,
    block_limit,
    out_weight,
    next_gain,
    next_weight,
):
    ring = Ring(lax.axis_size("ctx"), columns)
    rounds = ring.rounds
    queries, here = hidden.shape
    head_dim = q_gain.shape[0]
    heads_here = q_weight.shape[1] // head_dim
    rows = heads_here * queries
    kv_heads = key_cache.shape[1] // head_dim
    group_size = heads_here * 2 * ring.chips // kv_heads

    numbers = ring.locate(group_size // (2 * heads_here))

    row = jnp.arange(queries + 2, dtype=jnp.int32)[:, None]
    own = jnp.where(
        row < queries,
        jnp.pad(hidden, ((0, 2), (0, 0))),
        jnp.where(row == queries, attn_gain[None, :], next_gain[None, :]),
    )
    last = jnp.broadcast_to(block_limit[:, None], (queries, LANES))
    other = ring.swap(own)
    own, last = after(own, *numbers), after(last, *numbers)
    other_keys = ring.swap(after(key_cache, other))
    other_values = ring.swap(after(value_cache, other))
    cache = (key_cache, other_keys, value_cache, other_values)
    beside = {rounds - 1: (other_keys,), rounds: (other_values,)}

    def meanwhile(token):
        onehot, bias = prepare(ring, after(last, token), 2 * key_cache.shape[0])
        ready = after(key_cache, token), other_keys, after(value_cache, token), other_values
        return onehot, bias, *fetch(ring.number(0), ready)

    own_heads, carriers, (onehot, bias, *head) = gather_project(
        ring, queries, own, other, None, q_weight, beside, q_gain, meanwhile
    )
    other_weight = ring.swap(after(out_weight, own_heads))

    travelling, running, done = own_heads, None, own_heads
    for step in range(ring.chips):
        last = step + 1 == ring.chips
        if not last:
            coming = ring.send(travelling, 1)
        following = step + 1 if step < rounds else step + 1 - ring.chips
        (part,), head = attend(
            None if last else ring.number(following),
            after(travelling, done),
            1,
            bias,
            onehot,
            head,
            cache,
        )
        if step == 0:
            local = part
        else:
            running = ring.send(part if running is None else merge(rows, running, part), 1)
        travelling, done = coming, part
    attended = finish(rows, queries, (running, local))
    attended_other = ring.swap(attended)

    def mixed(kind, places):
        blocks = [ring.number(place) for place in places]
        weights = (out_weight, other_weight)
        parts = mix(blocks, here, kind, attended, attended_other, *weights)
        return dict(zip(places, parts))

    first = [(rounds, True), (rounds - 1, False)]
    places = [(step, mine) for step in range(rounds - 1, -1, -1) for mine in (True, False)]
    shares = mixed(BF16, first) | mixed(F32, [place for place in places if place not in first])
    own, other = (ring.send(shares[place], -1) for place in first)
    for step in range(rounds - 1, 0, -1):
        own = ring.send(add(shares[step, True], own), -1)
        if step > 1:
            other = ring.send(add(shares[step - 1, False], other), -1)
    own_far, other_far = ring.swap(own), ring.swap(other)
    new_own = add(shares[0, True], own, other_far, carriers[0, True])
    new_other = add(shares[0, False], other, own_far, carriers[0, False])
    next_queries, _, _ = gather_project(ring, queries, new_own, new_other, carriers, next_weight)
    return new_own, next_queries


def solution(mesh):
    in_specs = (
        P("groups", "ctx"),
        P("ctx"),
        P(None, "ctx"),
        P(),
        P(("groups", "ctx"), None),
        P(("groups", "ctx"), None),
        P("groups"),
        P("ctx", None),
        P("ctx"),
        P(None, "ctx"),
    )
    out_specs = (P("groups", "ctx"), P("groups", "ctx"))
    columns = 2 if mesh.shape["groups"] == 2 else 1
    return jax.shard_map(
        functools.partial(on_device, columns),
        mesh=mesh,
        in_specs=in_specs,
        out_specs=out_specs,
        check_vma=False,
    )
```

```python
import functools
import math

import jax
import jax.numpy as jnp
from jax import lax
from jax.experimental import pallas as pl
from jax.experimental.pallas import tpu as pltpu
from jax.sharding import PartitionSpec as P

BLK = 128
EPSILON = 1e-05
MASKED = -1e30
LANES = 128
TILE = 16
BF16 = jnp.bfloat16
F32 = jnp.float32
VMEM = pl.BlockSpec(memory_space=pltpu.VMEM)
ANYWHERE = pl.BlockSpec(memory_space=pl.ANY)
SCALARS = pl.BlockSpec(memory_space=pltpu.SMEM)


FREE = pl.CostEstimate(flops=0, bytes_accessed=0, transcendentals=0)


def took(microseconds):
    return pl.CostEstimate(
        flops=int(microseconds * 1.15e9), bytes_accessed=0, transcendentals=0
    )


class Ring:
    def __init__(self, devices, columns):
        self.chips = devices // 2
        self.rounds = self.chips // 2
        self.snake = columns == 2 and self.chips % 2 == 0
        if self.snake:
            self.order = list(range(0, self.chips, 2)) + list(range(1, self.chips, 2))[::-1]
        else:
            self.order = list(range(self.chips))

    def locate(self, key_share):
        device = lax.axis_index("ctx")
        two = jnp.int32(2)
        core, chip = lax.rem(device, two), lax.div(device, two)
        middle = self.chips // 2
        place = chip
        if self.snake:
            place = jnp.where(lax.rem(chip, two) == 0, lax.div(chip, two), self.chips - 1 - lax.div(chip, two))
        sign = 1 - 2 * lax.rem(core + place, two)
        names, values = ["self", "pair"], [device, device + 1 - 2 * core]
        for step in range(-self.rounds, self.rounds + 1):
            owner = lax.rem(place - sign * step + self.chips, jnp.int32(self.chips))
            if self.snake:
                owner = jnp.where(owner < middle, 2 * owner, 2 * (self.chips - 1 - owner) + 1)
            names += [(step, True), (step, False), step]
            half = core if step % 2 == 0 else 1 - core
            values += [2 * owner + half, 2 * owner + 1 - half, lax.div(owner, jnp.int32(key_share))]
        values = lax.optimization_barrier([x.astype(jnp.int32) for x in values])
        self.numbers = dict(zip(names, values))
        return values

    def number(self, name):
        return self.numbers[name].reshape(1)

    def send(self, block, way):
        route = []
        for place in range(self.chips):
            for core in (0, 1):
                ahead = way if (core + place) % 2 == 0 else -way
                to = self.order[(place + ahead) % self.chips]
                route.append((self.order[place] * 2 + core, to * 2 + 1 - core))
        return lax.ppermute(block, "ctx", sorted(route))

    def swap(self, block):
        return lax.ppermute(block, "ctx", [(i, i ^ 1) for i in range(2 * self.chips)])


def after(value, *others):
    return lax.optimization_barrier((value, *others))[0]


def near(x):
    return pltpu.with_memory_space_constraint(x, pltpu.VMEM)


def far(x):
    return pltpu.with_memory_space_constraint(x, pltpu.HBM)


def limit(megabytes):
    return pltpu.CompilerParams(vmem_limit_bytes=megabytes * 1024 * 1024)


def stat_rows(rows):
    return -(-3 * (rows // LANES) // TILE) * TILE


def diagonal():
    shape = (LANES, LANES)
    return lax.broadcasted_iota(jnp.int32, shape, 0) == lax.broadcasted_iota(jnp.int32, shape, 1)


def pack_stats(stats):
    high = [x.astype(BF16).astype(F32) for x in stats]
    rest = [x - h for x, h in zip(stats, high)]
    middle = [x.astype(BF16).astype(F32) for x in rest]
    low = [x - h for x, h in zip(rest, middle)]
    parts = high + middle + low
    parts += [jnp.zeros_like(stats[0])] * (-len(parts) % TILE)
    return jnp.concatenate(parts, axis=0).astype(BF16)


def unpack_stats(ref, rows):
    blocks = rows // LANES
    packed = ref[pl.ds(rows, stat_rows(rows)), :].astype(F32)
    return packed[:blocks] + packed[blocks : 2 * blocks] + packed[2 * blocks : 3 * blocks]


def fetch_columns(group, sources, targets, sems):
    columns = pl.ds(pl.multiple_of(group * LANES, LANES), LANES)
    tokens = sources[0].shape[0]
    copies = []
    for i, source in enumerate(sources):
        target = targets[i // 2].at[pl.ds((i % 2) * tokens, tokens), :]
        copies.append(pltpu.make_async_copy(source.at[:, columns], target, sems.at[i]))
        copies[-1].start()
    return copies


def prepare_kernel(this, pair, last, onehot, bias):
    shape = onehot.shape
    block = lax.broadcasted_iota(jnp.int32, shape, 0) // BLK
    lane = lax.broadcasted_iota(jnp.int32, shape, 1)
    onehot[...] = (block == lane).astype(F32).astype(BF16)
    blocks = shape[0] // BLK // 2
    lane = lax.broadcasted_iota(jnp.int32, bias.shape, 1)
    place = jnp.where(
        lane < blocks, this[0] * blocks + lane, (pair[0] - 1) * blocks + lane
    )
    bias[...] = jnp.where(place <= last[...], 0.0, MASKED).astype(BF16)


def prepare(ring, last, tokens):
    queries = last.shape[0]
    return pl.pallas_call(
        prepare_kernel,
        out_shape=[
            pltpu.VMEM((tokens, LANES), BF16),
            pltpu.VMEM((queries, LANES), BF16),
        ],
        in_specs=[SCALARS, SCALARS, VMEM],
        out_specs=[VMEM] * 2,
        compiler_params=limit(8),
        cost_estimate=took(0.09),
        name="prepare",
    )(ring.number("self"), ring.number("pair"), near(last))


def stage_kernel(source, target, sem):
    copy = pltpu.make_async_copy(source, target, sem)
    copy.start()
    copy.wait()


def stage(weight):
    return pl.pallas_call(
        stage_kernel,
        out_shape=pltpu.VMEM(weight.shape, weight.dtype),
        in_specs=[ANYWHERE],
        out_specs=VMEM,
        scratch_shapes=[pltpu.SemaphoreType.DMA],
        compiler_params=limit(8),
        cost_estimate=took(0.8999999999999999),
        name="stage",
    )(far(weight))


def fetch_kernel(head, k0, k1, v0, v1, key, value, sems):
    for copy in fetch_columns(head[0], (k0, k1, v0, v1), (key, value), sems):
        copy.wait()


def fetch(head, cache):
    shape = pltpu.VMEM((2 * cache[0].shape[0], LANES), BF16)
    return pl.pallas_call(
        fetch_kernel,
        out_shape=[shape, shape],
        in_specs=[SCALARS] + [ANYWHERE] * 4,
        out_specs=[VMEM] * 2,
        scratch_shapes=[pltpu.SemaphoreType.DMA((4,))],
        compiler_params=limit(8),
        cost_estimate=took(0.36),
        name="fetch",
    )(head, far(cache[0]), cache[1], far(cache[2]), cache[3])


def attend_kernel(chunk, parts, q, bias, onehot, key, value, *refs):
    copies = []
    if len(refs) > parts:
        following, *cache = refs[:5]
        outs, (next_key, next_value, sems) = refs[5 : 5 + parts], refs[5 + parts :]
        copies = fetch_columns(following[0], cache, (next_key, next_value), sems)
    else:
        outs = refs
    rows = q.shape[0] // parts
    diag = diagonal()
    biases = jnp.concatenate([bias[...]] * (chunk // bias.shape[0]), axis=0)

    def scores(start):
        query = jnp.concatenate([q[pl.ds(start, chunk), :], biases], axis=1)
        keys = jnp.concatenate([key[...], onehot[...]], axis=1)
        return lax.dot_general(
            query, keys, (((1,), (1,)), ((), ())), preferred_element_type=F32
        )

    starts = range(0, parts * rows, chunk)
    coming, stats = scores(0), []
    for start in starts:
        score = coming
        if start + chunk < parts * rows:
            coming = scores(start + chunk)
        peak = jnp.max(score, axis=1, keepdims=True)
        weights = jnp.exp2(score - peak).astype(BF16)
        values = jnp.concatenate([value[...], jnp.ones(value.shape, BF16)], axis=1)
        sums = jnp.dot(weights, values, preferred_element_type=F32)
        total = sums[:, LANES:]
        out, inside = outs[start // rows], start % rows
        out[pl.ds(inside, chunk), :] = (sums[:, :LANES] / total).astype(BF16)
        level = peak + jnp.log2(total)
        for b in range(chunk // LANES):
            block = level[b * LANES : (b + 1) * LANES]
            stats.append(jnp.sum(jnp.where(diag, block, 0.0), axis=0, keepdims=True))
        if inside + chunk == rows:
            out[pl.ds(rows, stat_rows(rows)), :] = pack_stats(stats)
            stats = []
    for copy in copies:
        copy.wait()


def attend(following, q, parts, bias, onehot, head, cache):
    rows, width = q.shape[0] // parts, q.shape[1]
    chunk = math.gcd(rows, 256)
    shapes = [pltpu.VMEM((rows + stat_rows(rows), width), BF16)] * parts
    arrays = [near(x) for x in (q, bias, onehot, *head)]
    specs, scratch = [VMEM] * 5, []
    if following is not None:
        shapes += [pltpu.VMEM(head[0].shape, BF16)] * 2
        arrays += [following, far(cache[0]), cache[1], far(cache[2]), cache[3]]
        specs += [SCALARS] + [ANYWHERE] * 4
        scratch = [pltpu.SemaphoreType.DMA((4,))]
    out = pl.pallas_call(
        functools.partial(attend_kernel, chunk, parts),
        out_shape=shapes,
        in_specs=specs,
        out_specs=[VMEM] * len(shapes),
        scratch_shapes=scratch,
        compiler_params=limit(16),
        cost_estimate=pl.CostEstimate(
            flops=32 * parts * rows * head[0].shape[0] * width,
            bytes_accessed=8 * head[0].size,
            transcendentals=parts * rows * head[0].shape[0],
        ),
        name="attend",
    )(*arrays)
    return out[:parts], out[parts:]


def spread(diag, row):
    high = row.astype(BF16).astype(F32)
    ones = jnp.ones((LANES, LANES), BF16)
    return sum(
        jnp.dot(jnp.where(diag, x, 0.0).astype(BF16), ones, preferred_element_type=F32)
        for x in (high, row - high)
    )


def merged(diag, block, one, one_stat, two, two_stat):
    peak = jnp.maximum(one_stat, two_stat)
    one_part, two_part = jnp.exp2(one_stat - peak), jnp.exp2(two_stat - peak)
    total = one_part + two_part
    share = spread(diag, one_part / total)
    here = pl.ds(block * LANES, LANES)
    one, two = one[here, :].astype(F32), two[here, :].astype(F32)
    return two + share * (one - two), peak + jnp.log2(total)


def merge_kernel(rows, one, two, out):
    diag = diagonal()
    one_stats, two_stats = unpack_stats(one, rows), unpack_stats(two, rows)
    stats = []
    for b in range(rows // LANES):
        value, stat = merged(diag, b, one, one_stats[b : b + 1], two, two_stats[b : b + 1])
        out[pl.ds(b * LANES, LANES), :] = value.astype(BF16)
        stats.append(stat)
    out[pl.ds(rows, stat_rows(rows)), :] = pack_stats(stats)


def merge(rows, one, two):
    return pl.pallas_call(
        functools.partial(merge_kernel, rows),
        out_shape=pltpu.VMEM(two.shape, BF16),
        in_specs=[VMEM, VMEM],
        out_specs=VMEM,
        cost_estimate=took(0.075),
        compiler_params=limit(8),
        name="merge",
    )(near(one), near(two))


def finish_kernel(rows, queries, *refs):
    parts, out = refs[:-1], refs[-1]
    diag = diagonal()
    width = parts[0].shape[1]
    stats = [unpack_stats(part, rows) for part in parts]
    for b in range(rows // LANES):
        here = pl.ds(b * LANES, LANES)
        levels = [stat[b : b + 1] for stat in stats]
        peak = functools.reduce(jnp.maximum, levels)
        shares = [jnp.exp2(level - peak) for level in levels]
        total = sum(shares)
        value = sum(
            spread(diag, share / total) * part[here, :].astype(F32)
            for share, part in zip(shares, parts)
        ).astype(BF16)
        for piece in range(LANES // queries):
            head = (b * LANES) // queries + piece
            out[:, pl.ds(head * width, width)] = value[piece * queries : (piece + 1) * queries]


def finish(rows, queries, parts):
    width = parts[0].shape[1]
    return pl.pallas_call(
        functools.partial(finish_kernel, rows, queries),
        out_shape=pltpu.VMEM((queries, rows // queries * width), BF16),
        in_specs=[VMEM] * len(parts),
        out_specs=VMEM,
        compiler_params=limit(8),
        cost_estimate=took(0.105),
        name="finish",
    )(*[near(x) for x in parts])


def weight_rows(weight, block, target, sem):
    width = target.shape[0]
    start = pl.multiple_of(block[0] * width, width)
    copy = pltpu.make_async_copy(weight.at[pl.ds(start, width), :], target, sem)
    copy.start()
    return copy


def project_kernel(plan, *refs):
    queries, features, scale, carried, begun, count, coming, fetched, resident = plan
    refs = list(refs)
    take = lambda n: [refs.pop(0) for _ in range(n)]
    blocks, later = take(0 if fetched else count), take(coming)
    parts = take(count)
    gains, row = (parts, queries) if carried else (take(count), queries + 1)
    weights = take(count) if fetched else take(1)
    state = take(2 if begun else 0)
    head_gain = take(1 if scale else 0)
    outs, targets = take(1 if features else 2), take(coming)
    copies = []
    if resident:
        depth = parts[0].shape[1]
        starts = [pl.multiple_of(block[0] * depth, depth) for block in blocks]
        weights_at, ahead = [weights[0].at[pl.ds(start, depth), :] for start in starts], []
    elif not fetched:
        pieces, sems = take(2)
        copies = [
            weight_rows(weights[0], block, pieces.at[i], sems.at[i])
            for i, block in enumerate(blocks)
        ]
        weights_at = [pieces.at[i] for i in range(count)]
        ahead = [
            weight_rows(weights[0], block, target, sems.at[count + i])
            for i, (block, target) in enumerate(zip(later, targets))
        ]
    else:
        weights_at, ahead = weights, []
    total, square = (state[0][...], state[1][...]) if begun else (0.0, 0.0)
    scaled = []
    for part, gain in zip(parts, gains):
        values = part[...][:queries].astype(F32)
        scaled.append((values * gain[...][row : row + 1].astype(F32)).astype(BF16))
        for lane in range(0, part.shape[1], LANES):
            square += values[:, lane : lane + LANES] * values[:, lane : lane + LANES]
    for i, weight in enumerate(weights_at):
        if copies:
            copies[i].wait()
        total += jnp.dot(scaled[i], weight[...], preferred_element_type=F32)
    if not features:
        outs[0][...] = total
        outs[1][...] = square
    else:
        factor = lax.rsqrt(jnp.sum(square, axis=1, keepdims=True) / features + EPSILON)
        if not scale:
            outs[0][...] = (total * factor).astype(BF16)
        else:
            gain = head_gain[0][...].astype(F32) * scale
            width = gain.shape[1]
            for head in range(total.shape[1] // width):
                value = total[:, head * width : (head + 1) * width] * factor
                mean = jnp.mean(value * value, axis=1, keepdims=True)
                outs[0][pl.ds(head * queries, queries), :] = (
                    value * lax.rsqrt(mean + EPSILON) * gain
                ).astype(BF16)
    for copy in ahead:
        copy.wait()


def project(queries, blocks, later, parts, gains, weight, state, fetched=None, last=False, head_gain=None, resident=False):
    count, depth, width = len(parts), parts[0].shape[1], weight.shape[1]
    scale = 0.0
    shapes = [pltpu.VMEM((queries, width), F32), pltpu.VMEM((queries, LANES), F32)]
    scalars = [] if fetched else [*blocks, *later]
    arrays = [near(x) for x in (*parts, *(gains or ()), *(fetched or ()))]
    specs = [VMEM] * len(arrays)
    if not fetched:
        arrays.append(near(weight) if resident else far(weight))
        specs.append(VMEM if resident else ANYWHERE)
    arrays += [near(x) for x in state or ()]
    if head_gain is not None:
        arrays.append(near(head_gain[None, :]))
        size = head_gain.shape[0]
        scale = size**-0.5 * math.log2(math.e)
        shapes = [pltpu.VMEM((width // size * queries, size), BF16)]
    elif last:
        shapes = [jax.ShapeDtypeStruct((queries, width), BF16)]
    specs += [VMEM] * (len(arrays) - len(specs))
    shapes += [pltpu.VMEM((depth, width), BF16)] * len(later)
    features = weight.shape[0] if last else 0
    plan = queries, features, scale, not gains, bool(state), count, len(later), bool(fetched), resident
    scratch = []
    if not fetched and not resident:
        scratch = [
            pltpu.VMEM((count, depth, width), BF16),
            pltpu.SemaphoreType.DMA((count + len(later),)),
        ]
    out = pl.pallas_call(
        functools.partial(project_kernel, plan),
        out_shape=shapes,
        in_specs=[SCALARS] * len(scalars) + specs,
        out_specs=[VMEM] * len(shapes),
        scratch_shapes=scratch,
        compiler_params=limit(16),
        cost_estimate=took(0.6),
        name="project",
    )(*scalars, *arrays)
    edge = len(out) - len(later)
    return out[:edge], out[edge:]


def gather_project(ring, queries, own, other, carriers, weight, beside=None, head_gain=None, meanwhile=None):
    arrived, waiting, state = {}, [], None
    rounds = ring.rounds
    final = [(rounds, True), (-rounds, False), (rounds - 1, False), (1 - rounds, True)]

    def flush(names, later=(), **how):
        waiting[:] = [name for name in waiting if name not in names]
        return project(
            queries,
            [ring.number(name) for name in names],
            [ring.number(name) for name in later],
            [arrived[name] for name in names],
            carriers and [carriers[name] for name in names],
            weight,
            state,
            resident=bool(carriers),
            **how,
        )

    def keep(name, part):
        arrived[name] = part
        waiting.append(name)

    keep((0, True), own)
    keep((0, False), other)
    for step in range(1, rounds + 1):
        own = ring.send(after(own, *(beside or {}).get(step, ()), *(state or ())), 1)
        if step < rounds:
            other = ring.send(other, 1)
            if len(waiting) > 16:
                state, _ = flush([name for name in waiting if abs(name[0]) < step - 1])
            keep((step, True), own)
            keep((-step, False), ring.swap(own))
            keep((step, False), other)
            if step < rounds - 1:
                keep((-step, True), ring.swap(other))
    state, fetched = flush([name for name in waiting if name not in final], () if carriers else final)
    before = arrived[rounds - 1, True]
    own, other, before = after(own, *state), after(other, own, *state), after(before, own, *state)
    extra = meanwhile(own) if meanwhile else ()
    keep((rounds, True), own)
    keep((-rounds, False), after(ring.swap(own), *extra))
    keep((1 - rounds, True), ring.swap(other))
    (result,), _ = flush(final, fetched=fetched, last=True, head_gain=head_gain)
    return result, arrived, extra


def mix_kernel(count, *refs):
    blocks, (one, two, one_weight, two_weight) = refs[:count], refs[count : count + 4]
    for block, out in zip(blocks, refs[count + 4 :]):
        width = out.shape[1]
        columns = pl.ds(pl.multiple_of(block[0] * width, width), width)
        value = jnp.dot(one[...], one_weight[:, columns], preferred_element_type=F32)
        value += jnp.dot(two[...], two_weight[:, columns], preferred_element_type=F32)
        out[...] = value.astype(out.dtype)


def mix(blocks, width, kind, one, two, one_weight, two_weight):
    return pl.pallas_call(
        functools.partial(mix_kernel, len(blocks)),
        out_shape=[pltpu.VMEM((one.shape[0], width), kind)] * len(blocks),
        in_specs=[SCALARS] * len(blocks) + [VMEM] * 4,
        out_specs=[VMEM] * len(blocks),
        compiler_params=limit(8),
        cost_estimate=took(0.18),
        name="mix",
    )(*blocks, *[near(x) for x in (one, two, one_weight, two_weight)])


def add_kernel(*refs):
    rows = refs[-1].shape[0]
    refs[-1][...] = sum(ref[...][:rows].astype(F32) for ref in refs[:-1]).astype(BF16)


def add(*parts):
    return pl.pallas_call(
        add_kernel,
        out_shape=pltpu.VMEM(parts[0].shape, BF16),
        in_specs=[VMEM] * len(parts),
        out_specs=VMEM,
        compiler_params=limit(8),
        cost_estimate=took(0.03),
        name="add",
    )(*[near(x) for x in parts])


def join_kernel(one, two, out):
    rows = one.shape[0]
    out[:rows] = one[...]
    out[rows:] = two[...]


def join(one, two):
    return pl.pallas_call(
        join_kernel,
        out_shape=pltpu.VMEM((2 * one.shape[0], one.shape[1]), one.dtype),
        in_specs=[VMEM, VMEM],
        out_specs=VMEM,
        compiler_params=limit(8),
        cost_estimate=took(0.03),
        name="join",
    )(near(one), near(two))


def first_half_kernel(both, out):
    out[...] = both[: out.shape[0]]


def first_half(both):
    return pl.pallas_call(
        first_half_kernel,
        out_shape=pltpu.VMEM((both.shape[0] // 2, both.shape[1]), both.dtype),
        in_specs=[VMEM],
        out_specs=VMEM,
        compiler_params=limit(8),
        cost_estimate=took(0.03),
        name="first_half",
    )(near(both))


def on_device(
    columns,
    hidden,
    attn_gain,
    q_weight,
    q_gain,
    key_cache,
    value_cache,
    block_limit,
    out_weight,
    next_gain,
    next_weight,
):
    ring = Ring(lax.axis_size("ctx"), columns)
    rounds = ring.rounds
    queries, here = hidden.shape
    head_dim = q_gain.shape[0]
    heads_here = q_weight.shape[1] // head_dim
    rows = heads_here * queries
    kv_heads = key_cache.shape[1] // head_dim
    group_size = heads_here * 2 * ring.chips // kv_heads

    numbers = ring.locate(group_size // (2 * heads_here))

    row = jnp.arange(queries + 2, dtype=jnp.int32)[:, None]
    own = jnp.where(
        row < queries,
        jnp.pad(hidden, ((0, 2), (0, 0))),
        jnp.where(row == queries, attn_gain[None, :], next_gain[None, :]),
    )
    last = jnp.broadcast_to(block_limit[:, None], (queries, LANES))
    other = ring.swap(own)
    own, last = after(own, *numbers), after(last, *numbers)
    other_keys = ring.swap(after(key_cache, other))
    other_values = ring.swap(after(value_cache, other))
    cache = (key_cache, other_keys, value_cache, other_values)
    onehot, bias = prepare(ring, last, 2 * key_cache.shape[0])
    beside = {2: (onehot, bias), rounds - 1: (other_keys,), rounds: (other_values,)}

    def meanwhile(token):
        ready = after(key_cache, token), other_keys, after(value_cache, token), other_values
        return fetch(ring.number(0), ready)

    own_heads, carriers, head = gather_project(
        ring, queries, own, other, None, q_weight, beside, q_gain, meanwhile
    )
    other_weight = ring.swap(after(out_weight, own_heads))

    travelling, running, done = own_heads, None, own_heads
    for step in range(ring.chips):
        last = step + 1 == ring.chips
        if not last:
            coming = ring.send(travelling, 1)
        following = step + 1 if step < rounds else step + 1 - ring.chips
        (part,), head = attend(
            None if last else ring.number(following),
            after(travelling, done),
            1,
            bias,
            onehot,
            head,
            cache,
        )
        if step == 0:
            local = part
        else:
            running = ring.send(part if running is None else merge(rows, running, part), 1)
        travelling, done = coming, part
    attended = finish(rows, queries, (running, local))
    attended_other = ring.swap(attended)

    def mixed(kind, places):
        blocks = [ring.number(place) for place in places]
        weights = (out_weight, other_weight)
        parts = mix(blocks, here, kind, attended, attended_other, *weights)
        return dict(zip(places, parts))

    first = [(rounds, True), (rounds - 1, False)]
    places = [(step, mine) for step in range(rounds - 1, -1, -1) for mine in (True, False)]
    shares = mixed(BF16, first) | mixed(F32, [place for place in places if place not in first])
    own, other = (ring.send(shares[place], -1) for place in first)
    for step in range(rounds - 1, 0, -1):
        own = ring.send(add(shares[step, True], own), -1)
        if step > 1:
            other = ring.send(add(shares[step - 1, False], other), -1)
    own_far, other_far = ring.swap(own), ring.swap(other)
    new_own = add(shares[0, True], own, other_far, carriers[0, True])
    new_other = add(shares[0, False], other, own_far, carriers[0, False])
    next_queries, _, _ = gather_project(ring, queries, new_own, new_other, carriers, next_weight)
    return new_own, next_queries


def solution(mesh):
    in_specs = (
        P("groups", "ctx"),
        P("ctx"),
        P(None, "ctx"),
        P(),
        P(("groups", "ctx"), None),
        P(("groups", "ctx"), None),
        P("groups"),
        P("ctx", None),
        P("ctx"),
        P(None, "ctx"),
    )
    out_specs = (P("groups", "ctx"), P("groups", "ctx"))
    columns = 2 if mesh.shape["groups"] == 2 else 1
    return jax.shard_map(
        functools.partial(on_device, columns),
        mesh=mesh,
        in_specs=in_specs,
        out_specs=out_specs,
        check_vma=False,
    )
```
